256 devices in a mesh: stream: 4 (over x), cy: 8 (over y, core), cz: 8 (over z).
Axes of the slice: x: 4, y: 4, z: 8, core: 2. Of those that a mesh axis runs over, the one named last changes fastest.
Arguments:
- state: float32 [5, 8, 128, 1024], P(None, 'stream', 'cy', 'cz'), may hold values from -3 to 3
- source: float32 [5, 8, 128, 1024], P(None, 'stream', 'cy', 'cz'), may hold values from -3 to 3
- diag_scale: float32 [5, 8, 128, 1024], P(None, 'stream', 'cy', 'cz'), may hold values from 1.5 to 3
- diag_inverse: float32 [5, 5, 8, 128, 1024], P(None, None, 'stream', 'cy', 'cz'), may hold values from -0.1 to 0.9
- couple: float32 [7, 5, 5], replicated, may hold values from -2 to 2
- fluid: int32 [8, 128, 1024], P('stream', 'cy', 'cz'), may hold values 0 or 1
- donor_index: int32 [4, 8, 8, 64, 256], P('stream', 'cy', 'cz'), may hold values from 0 to 4095
- donor_count: int32 [4, 8, 8, 64], P('stream', 'cy', 'cz'), may hold values from 0 to 256, as said below
- ghost_cell: int32 [4, 8, 8, 1024], P('stream', 'cy', 'cz'), may hold values from 0 to 4095, as said below
- ghost_source: int32 [4, 8, 8, 1024, 8], P('stream', 'cy', 'cz'), may hold values from 0 to 16383
- ghost_weight: float32 [4, 8, 8, 1024, 8], P('stream', 'cy', 'cz'), may hold values from 0.02 to 0.25
Outputs:
- new_state: float32 [5, 8, 128, 1024], P(None, 'stream', 'cy', 'cz')
The draws below stay inside these ranges and needn't reach their ends.
Inputs may be any that keep to these rules, and one draw needn't show every extreme that they name: donor_count counts the live leading slots; every device has one destination whose 256 slots are all live. `ghost_cell`: the ghost cells of one device are distinct local cells.
All inputs are finite; a program needn't handle non-finite values. No bound on the sum of `fluid` on one device may be relied on, other than what follows from the above.
Results may differ from the reference program's by a relative error of at most 0.0001.
Values sent between devices are 32-bit elements; how exact they have to be, the bound alone decides.
No kernel may reach another device: no remote copies, remote signals or barrier semaphores. Data moves between devices by JAX's collectives and lax.ppermute only.
A program may use at most 64 MiB of HBM per device.

```python
import math
import jax
import jax.numpy as jnp
from jax import lax

NVAR = 5
CX = 2
CY = 16
CZ = 128
SLOTS = 256
NG = 1024
KDON = 8
CELLS = 4096
GROUP = 64
NX = 8
NY = 128
NZ = 1024
N_STREAM = 4
N_CY = 8
N_CZ = 8


def draw_rates(key):
    base = jax.random.fold_in(key, 7)
    keys = jax.random.split(base, 7)
    weighted_routine = jax.random.uniform(keys[0], (NVAR,), jnp.float32, 0.5, 0.8)
    keep_lower = jnp.exp(jax.random.uniform(keys[1], (NVAR,), jnp.float32, math.log(0.25), math.log(0.6)) / NX)
    keep_upper = jnp.exp(jax.random.uniform(keys[2], (NVAR,), jnp.float32, math.log(0.25), math.log(0.6)) / NX)
    fast_lower = jax.random.uniform(keys[3], (NVAR,), jnp.float32, 0.3, 0.6)
    fast_upper = jax.random.uniform(keys[4], (NVAR,), jnp.float32, 0.3, 0.6)
    rank_lower = jax.random.permutation(keys[5], NVAR)
    rank_upper = jax.random.permutation(keys[6], NVAR)
    slow_lower = (NVAR + 1) // 2
    slow_upper = (NVAR + 1) // 2
    rate_lower = jnp.where(rank_lower < slow_lower, keep_lower, fast_lower)
    rate_upper = jnp.where(rank_upper < slow_upper, keep_upper, fast_upper)
    return (weighted_routine, rate_lower, rate_upper)


def draw_diag_inverse(key, part):
    weighted_routine, rate_lower, rate_upper = draw_rates(key)
    own_key = jax.random.fold_in(key, 11)
    first, second, third, fourth = jax.random.split(own_key, 4)
    rough_guess = jnp.exp(jax.random.uniform(first, (NVAR, NX, NY, NZ), jnp.float32, -0.1, 0.1))
    match_tally = jax.random.randint(second, (NX,), 0, NX) < 2
    discarded_entry = jax.random.uniform(third, (NX,), jnp.float32, 0.5, 0.8)
    message_span = jnp.where(match_tally, discarded_entry, jnp.ones_like(discarded_entry))
    execute_routine = weighted_routine[:, None, None, None] * rough_guess * message_span[None, :, None, None]
    off = jnp.clip(0.035 * jax.random.normal(fourth, (NVAR, NVAR, NX, NY, NZ), jnp.float32), -0.1, 0.1)
    unit = jnp.eye(NVAR, dtype=jnp.float32)[:, :, None, None, None]
    return unit * execute_routine[None] + (1.0 - unit) * off


def draw_couple(key, part):
    weighted_routine, rate_lower, rate_upper = draw_rates(key)
    own_key = jax.random.fold_in(key, 13)
    first, second = jax.random.split(own_key)
    base = jnp.clip(0.12 * jax.random.normal(first, (7, NVAR, NVAR), jnp.float32), -0.4, 0.4)
    link = jnp.clip(0.02 * jax.random.normal(second, (2, NVAR, NVAR), jnp.float32), -0.06, 0.06)
    unit = jnp.eye(NVAR, dtype=jnp.float32)
    lower_link = unit * (rate_lower / weighted_routine)[None, :] + (1.0 - unit) * link[0]
    upper_link = -unit * (rate_upper / weighted_routine)[None, :] + (1.0 - unit) * link[1]
    return base.at[1].set(lower_link).at[2].set(upper_link)


def draw_donor_count(key, part):
    key = jax.random.fold_in(key, 17)
    first, second, third = jax.random.split(key, 3)
    raw = jax.random.randint(first, (N_STREAM, N_CY, N_CZ, GROUP), 0, SLOTS + 1)
    level = jax.random.randint(second, (N_STREAM, N_CY, N_CZ, 1), 1, 5)
    count = jnp.minimum(SLOTS, raw * level // 2)
    full = jax.random.randint(third, (N_STREAM, N_CY, N_CZ, 1), 0, GROUP)
    dest = jnp.arange(GROUP, dtype=jnp.int32)
    return jnp.where(dest[None, None, None, :] == full, SLOTS, count).astype(jnp.int32)


def draw_ghost_cell(key, part):
    key = jax.random.fold_in(key, 19)
    scores = jax.random.randint(key, (N_STREAM, N_CY, N_CZ, CELLS), 0, 16384)
    distinct = scores * CELLS + jnp.arange(CELLS, dtype=jnp.int32)
    order = jnp.argsort(distinct, axis=-1)
    return order[..., :NG].astype(jnp.int32)


def place_ends(array, key, low, high):
    shape = array.shape
    index_at = [jax.random.randint(jax.random.fold_in(key, axis), (), 0, shape[axis]) for axis in range(len(shape))]
    array = array.at[tuple(index_at)].set(low)
    longest = shape.index(max(shape))
    index_at[longest] = (index_at[longest] + 1) % shape[longest]
    return array.at[tuple(index_at)].set(high)


def block_scale(rng, dims, cuts, least, largest):
    gain, own = 1.0, jax.random.fold_in(rng, 6)
    for axis_at, blocks in cuts:
        steps = jnp.exp(jax.random.uniform(jax.random.fold_in(own, axis_at), (blocks,), jnp.float32, least / len(cuts), largest / len(cuts)))
        gain = gain * jnp.repeat(steps, dims[axis_at] // blocks).reshape([-1 if axis == axis_at else 1 for axis in range(len(dims))])
    return gain


def gaussian(stream_key, dims, width, bound, pieces=(), kind=jnp.bfloat16):
    level = block_scale(stream_key, dims, pieces, -0.22, 0.18) if pieces else 1.0
    values = jax.random.normal(stream_key, dims, jnp.float32) * width * level
    return jnp.minimum(jnp.maximum(values, -bound), bound).astype(kind)


def setup_inputs(seed: int = 0) -> dict:
    key_of = jax.random.split(jax.random.key(seed), 12)
    state = gaussian(key_of[0], (NVAR, NX, NY, NZ), 0.5, 3.0, ((1, 4), (2, 8), (3, 8)), jnp.float32)
    source = gaussian(key_of[1], (NVAR, NX, NY, NZ), 0.5, 3.0, ((1, 4), (2, 8), (3, 8)), jnp.float32)
    diag_scale = jnp.clip(jnp.exp(math.log(3.0) - 0.6931472 * jax.random.uniform(key_of[2], (NVAR, NX, NY, NZ), jnp.float32) ** block_scale(key_of[2], (NVAR, NX, NY, NZ), ((1, 4), (2, 8), (3, 8)), -0.2, 0.2)), 1.5, 3.0)
    diag_inverse = draw_diag_inverse(jax.random.fold_in(key_of[11], 71), 0)
    couple = draw_couple(jax.random.fold_in(key_of[11], 71), 0)
    fluid = place_ends((jax.random.randint(key_of[5], (NX, NY, NZ), 0, 8) < 7).astype(jnp.int32), jax.random.fold_in(key_of[5], 1), 0, 1)
    donor_index = place_ends(jax.random.randint(key_of[6], (N_STREAM, N_CY, N_CZ, GROUP, SLOTS), 0, CELLS), jax.random.fold_in(key_of[6], 1), 0, CELLS - 1).astype(jnp.int32)
    donor_count = draw_donor_count(jax.random.fold_in(key_of[11], 71), 0)
    ghost_cell = draw_ghost_cell(jax.random.fold_in(key_of[11], 71), 0)
    ghost_source = place_ends(jax.random.randint(key_of[9], (N_STREAM, N_CY, N_CZ, NG, KDON), 0, GROUP * SLOTS), jax.random.fold_in(key_of[9], 1), 0, (GROUP * SLOTS) - 1).astype(jnp.int32)
    ghost_weight = jnp.clip(0.02 + 0.23 * jax.random.uniform(key_of[10], (N_STREAM, N_CY, N_CZ, NG, KDON), jnp.float32) ** block_scale(key_of[10], (N_STREAM, N_CY, N_CZ, NG, KDON), ((0, 4), (1, 8), (2, 8)), -0.2, 0.2), 0.02, 0.25)
    return dict(state=state, source=source, diag_scale=diag_scale, diag_inverse=diag_inverse, couple=couple, fluid=fluid, donor_index=donor_index, donor_count=donor_count, ghost_cell=ghost_cell, ghost_source=ghost_source, ghost_weight=ghost_weight)


HIGH = lax.Precision.HIGHEST
RELAX = 0.8


def apply_block(matrix, field):
    return jnp.einsum('ij,j...->i...', matrix, field, precision=HIGH)


def cell_apply(pmat, vector):
    return jnp.sum(pmat * vector[None], axis=1)


def reference(state, source, diag_scale, diag_inverse, couple, fluid, donor_index, donor_count, ghost_cell, ghost_source, ghost_weight):
    devs = N_STREAM * N_CY * N_CZ
    blocks = state.reshape(NVAR, N_STREAM, CX, N_CY, CY, N_CZ, CZ).transpose(1, 3, 5, 0, 2, 4, 6).reshape(devs, NVAR, CELLS)
    picked = jax.vmap(lambda blk, idx: blk[:, idx])(blocks, donor_index.reshape(devs, GROUP * SLOTS))
    slot_ids = jnp.arange(SLOTS, dtype=jnp.int32)
    live = (slot_ids[None, None, :] < donor_count.reshape(devs, GROUP)[:, :, None]).reshape(devs, 1, GROUP * SLOTS)
    sent = jnp.where(live, picked, jnp.zeros_like(picked)).reshape(N_STREAM, GROUP, NVAR, GROUP, SLOTS)
    received = sent.transpose(0, 3, 2, 1, 4).reshape(devs, NVAR, GROUP * SLOTS)
    values = jax.vmap(lambda rec, idx: rec[:, idx])(received, ghost_source.reshape(devs, NG * KDON)).reshape(devs, NVAR, NG, KDON)
    ghost_value = jnp.sum(values * ghost_weight.reshape(devs, 1, NG, KDON), axis=-1)
    filled_blocks = jax.vmap(lambda blk, cell, val: blk.at[:, cell].set(val))(blocks, ghost_cell.reshape(devs, NG), ghost_value)
    populated_ghosts = filled_blocks.reshape(N_STREAM, N_CY, N_CZ, NVAR, CX, CY, CZ).transpose(3, 0, 4, 1, 5, 2, 6).reshape(NVAR, NX, NY, NZ)
    padded = jnp.pad(populated_ghosts, ((0, 0), (1, 1), (1, 1), (1, 1)))
    near = [padded[:, :-2, 1:-1, 1:-1], padded[:, 2:, 1:-1, 1:-1],
            padded[:, 1:-1, :-2, 1:-1], padded[:, 1:-1, 2:, 1:-1],
            padded[:, 1:-1, 1:-1, :-2], padded[:, 1:-1, 1:-1, 2:]]
    image = diag_scale * populated_ghosts + apply_block(couple[0], populated_ghosts)
    for direction in range(6):
        image = image + apply_block(couple[direction + 1], near[direction])
    maskf = fluid.astype(jnp.float32)
    residual = maskf[None] * (source - image)
    inv_planes = jnp.moveaxis(diag_inverse, 2, 0)
    res_planes = jnp.moveaxis(residual, 1, 0)
    zero = jnp.zeros((NVAR, NY, NZ), jnp.float32)

    def lower_step(prev, xs):
        pmat, rhs = xs
        cur = cell_apply(pmat, rhs - apply_block(couple[1], prev))
        return cur, cur

    _, lower = lax.scan(lower_step, zero, (inv_planes, res_planes))

    def upper_step(prev, xs):
        pmat, low = xs
        cur = low - cell_apply(pmat, apply_block(couple[2], prev))
        return cur, cur

    _, upper = lax.scan(upper_step, zero, (inv_planes, lower), reverse=True)
    return populated_ghosts + RELAX * maskf[None] * jnp.moveaxis(upper, 0, 1)
```

```python
import jax
import jax.numpy as jnp
from jax import lax
from jax.experimental import pallas as pl
from jax.experimental.pallas import tpu as pltpu
from jax.sharding import PartitionSpec as P

RELAX = 0.8
LANES = 128
F32 = jnp.float32
BF16 = jnp.bfloat16
VMEM = pl.BlockSpec(memory_space=pltpu.VMEM)
SMEM = pl.BlockSpec(memory_space=pltpu.SMEM)
BYTES = 24 << 20


def ring(x, axis, steps):
    count = lax.axis_size(axis)
    return lax.ppermute(x, axis, [(i, (i + steps) % count) for i in range(count)])


def call(kernel, outs, args, specs, name):
    return pl.pallas_call(
        kernel,
        out_shape=outs,
        in_specs=specs,
        out_specs=jax.tree.map(lambda _: VMEM, outs),
        name=name,
        compiler_params=pltpu.CompilerParams(vmem_limit_bytes=BYTES),
    )(*args)


def lane_pick(rows, lane):
    return jnp.take_along_axis(rows, lane, axis=1, mode="promise_in_bounds")


def donor_kernel(idx_ref, count_ref, state_ref, out_ref):
    lanes = lax.broadcasted_iota(jnp.int32, (8, LANES), 1)
    subs = lax.broadcasted_iota(jnp.int32, (8, LANES), 0)

    def body(g, carry):
        base = pl.multiple_of(g * 8, 8)
        count = jnp.zeros((8, LANES), jnp.int32)
        for q in range(8):
            count = jnp.where(subs == q, count_ref[0, g * 8 + q], count)
        for h in range(2):
            idx = idx_ref[pl.ds(base, 8), h * LANES : (h + 1) * LANES]
            lane = idx & (LANES - 1)
            row = idx >> 7
            acc = [jnp.zeros((8, LANES), F32) for _ in range(5)]
            for r in range(32):
                hit = row == r
                for v in range(5):
                    line = state_ref[v * 32 + r : v * 32 + r + 1, :]
                    line = jnp.broadcast_to(line, (8, LANES))
                    acc[v] = jnp.where(hit, lane_pick(line, lane), acc[v])
            live = lanes + h * LANES < count
            for v in range(5):
                at = (v * 2 + h) * LANES
                out_ref[pl.ds(base, 8), 0, at : at + LANES] = jnp.where(live, acc[v], 0.0)
        return carry

    lax.fori_loop(0, 8, body, 0)


def ghost_kernel(
    rec_ref, src_ref, w_ref, cell_ref, state_ref, f_ref, x0_ref, x1_ref, y_ref, z_ref
):
    tabs = []
    for v in range(5):
        t = rec_ref[:, 0, v * 256 : (v + 1) * 256]
        hi = t.astype(BF16)
        lo = (t - hi.astype(F32)).astype(BF16)
        tabs.append(jnp.concatenate([hi, lo], axis=1))
    tab = jnp.concatenate(tabs, axis=0)
    width = 256
    lane_ids = lax.broadcasted_iota(jnp.int32, (256, width), 0)
    row_ids = lax.broadcasted_iota(jnp.int32, (64, width), 0)
    parts = [[] for _ in range(5)]
    for j in range(1024 // width):
        at = slice(j * width, (j + 1) * width)
        acc = [jnp.zeros((8, width), F32) for _ in range(5)]
        for k in range(8):
            entry = src_ref[k : k + 1, at]
            weight = w_ref[k : k + 1, at]
            onehot = (lane_ids == (entry & 255)).astype(BF16)
            onehot = jnp.concatenate([onehot, onehot], axis=0)
            p = jnp.dot(tab, onehot, preferred_element_type=F32)
            m = jnp.where(row_ids == (entry >> 8), weight, 0.0)
            for v in range(5):
                q = p[v * 64 : (v + 1) * 64] * m
                acc[v] = acc[v] + jnp.sum(q.reshape(8, 8, width), axis=0)
        for v in range(5):
            parts[v].append(jnp.sum(acc[v], axis=0, keepdims=True))
    values = [jnp.concatenate(p, axis=1) for p in parts]

    cell = cell_ref[...]
    in_row = lax.broadcasted_iota(jnp.int32, (32, 1024), 0) == (cell >> 7)
    in_lane = lax.broadcasted_iota(jnp.int32, (LANES, 1024), 0) == (cell & (LANES - 1))
    pieces = [[], [], []]
    for v in range(5):
        x = jnp.where(in_row, values[v], 0.0)
        hi = x.astype(BF16)
        rest = x - hi.astype(F32)
        mid = rest.astype(BF16)
        pieces[0].append(hi)
        pieces[1].append(mid)
        pieces[2].append((rest - mid.astype(F32)).astype(BF16))
    left = jnp.concatenate([in_row.astype(BF16)] + pieces[0] + pieces[1] + pieces[2], axis=0)
    placed = lax.dot_general(
        left, in_lane.astype(BF16), (((1,), (1,)), ((), ())), preferred_element_type=F32
    )
    covered = placed[0:32] > 0.5
    diag = lax.broadcasted_iota(jnp.int32, (16, LANES), 0) == lax.broadcasted_iota(
        jnp.int32, (16, LANES), 1
    )
    for v in range(5):
        hi, mid, lo = (placed[32 * (1 + v + 5 * p) : 32 * (2 + v + 5 * p)] for p in range(3))
        old = state_ref[32 * v : 32 * v + 32, :]
        new = jnp.where(covered, hi + (mid + lo), old)
        f_ref[32 * v : 32 * v + 32, :] = new
        x0_ref[v] = new[0:16]
        x1_ref[v] = new[16:32]
        for x in range(2):
            plane = new[16 * x : 16 * x + 16]
            row = 2 * v + x
            y_ref[0, row : row + 1, :] = plane[0:1]
            y_ref[1, row : row + 1, :] = plane[15:16]
            for side, col in ((0, 0), (1, LANES - 1)):
                face = jnp.where(diag, plane[:, col : col + 1], 0.0)
                z_ref[side, row : row + 1, :] = jnp.sum(face, axis=0, keepdims=True)


def residual_kernel(
    f_ref, xm_ref, xp_ref, ym_ref, yp_ref, zm_ref, zp_ref, source_ref, scale_ref, fluid_ref,
    couple_ref, out_ref,
):
    s, a, b = (lax.axis_index(n) for n in ("stream", "cy", "cz"))
    ns, na, nb = (lax.axis_size(n) for n in ("stream", "cy", "cz"))
    shape = (16, LANES)
    subs = lax.broadcasted_iota(jnp.int32, shape, 0)
    lanes = lax.broadcasted_iota(jnp.int32, shape, 1)

    def column(ref, row):
        line = jnp.broadcast_to(ref[row : row + 1, :], shape)
        return jnp.concatenate(
            [lane_pick(line[0:8], subs[0:8]), lane_pick(line[8:16], subs[8:16])], axis=0
        )

    for x in range(2):
        near = [[] for _ in range(7)]
        for v in range(5):
            row = 2 * v + x
            mid = f_ref[32 * v + 16 * x : 32 * v + 16 * x + 16, :]
            other = f_ref[32 * v + 16 * (1 - x) : 32 * v + 16 * (1 - x) + 16, :]
            if x == 0:
                xm, xp = jnp.where(s > 0, xm_ref[v], 0.0), other
            else:
                xm, xp = other, jnp.where(s < ns - 1, xp_ref[v], 0.0)
            ym = jnp.where(a > 0, ym_ref[row : row + 1, :], 0.0)
            yp = jnp.where(a < na - 1, yp_ref[row : row + 1, :], 0.0)
            zm = jnp.where(b > 0, column(zm_ref, row), 0.0)
            zp = jnp.where(b < nb - 1, column(zp_ref, row), 0.0)
            near[0].append(mid)
            near[1].append(xm)
            near[2].append(xp)
            near[3].append(jnp.where(subs == 0, ym, pltpu.roll(mid, 1, 0)))
            near[4].append(jnp.where(subs == 15, yp, pltpu.roll(mid, 15, 0)))
            near[5].append(jnp.where(lanes == 0, zm, pltpu.roll(mid, 1, 1)))
            near[6].append(jnp.where(lanes == LANES - 1, zp, pltpu.roll(mid, LANES - 1, 1)))
        wet = fluid_ref[x].astype(F32)
        for i in range(5):
            image = scale_ref[i, x] * near[0][i]
            for d in range(7):
                for j in range(5):
                    image = image + couple_ref[d, i, j] * near[d][j]
            out_ref[x, i] = wet * (source_ref[i, x] - image)


def sweep_kernel(
    res_ref, prev_ref, next_ref, far_ref, inv_ref, f_ref, fluid_ref, couple_ref, out_ref, low_ref
):
    s = lax.axis_index("stream")
    count = 4
    zero = jnp.zeros((16, LANES), F32)
    prev = [zero] * 5
    for q in range(count):
        o = lax.rem(q - s + count, count)
        for x in range(2):
            t = []
            for i in range(5):
                r = jnp.where(
                    o == 0,
                    res_ref[x, i],
                    jnp.where(
                        o == 1, next_ref[x, i], jnp.where(o == 2, far_ref[x, i], prev_ref[x, i])
                    ),
                )
                for j in range(5):
                    r = r - couple_ref[1, i, j] * prev[j]
                t.append(r)
            cur = []
            for i in range(5):
                c = inv_ref[o, i, 0, x] * t[0]
                for j in range(1, 5):
                    c = c + inv_ref[o, i, j, x] * t[j]
                cur.append(c)
                low_ref[2 * q + x, i] = c
            prev = cur
    prev = [zero] * 5
    for q in reversed(range(count)):
        o = lax.rem(q - s + count, count)
        for x in (1, 0):
            t = []
            for i in range(5):
                r = couple_ref[2, i, 0] * prev[0]
                for j in range(1, 5):
                    r = r + couple_ref[2, i, j] * prev[j]
                t.append(r)
            cur = []
            for i in range(5):
                c = low_ref[2 * q + x, i]
                for j in range(5):
                    c = c - inv_ref[o, i, j, x] * t[j]
                cur.append(c)
            prev = cur

            @pl.when(o == 0)
            def _():
                wet = RELAX * fluid_ref[x].astype(F32)
                for i in range(5):
                    at = 32 * i + 16 * x
                    out_ref[i, x] = f_ref[at : at + 16, :] + wet * cur[i]


def on_device(
    state,
    source,
    diag_scale,
    diag_inverse,
    couple,
    fluid,
    donor_index,
    donor_count,
    ghost_cell,
    ghost_source,
    ghost_weight,
):
    table = state.reshape(160, LANES)
    sent = call(
        donor_kernel,
        jax.ShapeDtypeStruct((64, 1, 1280), F32),
        (donor_index.reshape(64, 256), donor_count.reshape(1, 64), table),
        [VMEM, SMEM, VMEM],
        "donor_pick",
    )
    received = lax.all_to_all(sent, ("cy", "cz"), split_axis=0, concat_axis=0, tiled=True)
    inv = jnp.stack(
        [diag_inverse] + [ring(diag_inverse, "stream", step) for step in (-1, 2, 1)]
    )
    plane = jax.ShapeDtypeStruct((5, 16, LANES), F32)
    faces = jax.ShapeDtypeStruct((2, 10, LANES), F32)
    filled, first, last, yface, zface = call(
        ghost_kernel,
        (jax.ShapeDtypeStruct((160, LANES), F32), plane, plane, faces, faces),
        (
            received,
            ghost_source.reshape(1024, 8).T,
            ghost_weight.reshape(1024, 8).T,
            ghost_cell.reshape(1, 1024),
            table,
        ),
        [VMEM] * 5,
        "ghost_fill",
    )
    xm, xp = ring(last, "stream", 1), ring(first, "stream", -1)
    ym, yp = ring(yface[1], "cy", 1), ring(yface[0], "cy", -1)
    zm, zp = ring(zface[1], "cz", 1), ring(zface[0], "cz", -1)
    residual = call(
        residual_kernel,
        jax.ShapeDtypeStruct((2, 5, 16, LANES), F32),
        (filled, xm, xp, ym, yp, zm, zp, source, diag_scale, fluid, couple),
        [VMEM] * 10 + [SMEM],
        "residual",
    )
    after, far, before = (ring(residual, "stream", step) for step in (-1, 2, 1))
    return pl.pallas_call(
        sweep_kernel,
        out_shape=jax.ShapeDtypeStruct((5, 2, 16, LANES), F32),
        in_specs=[VMEM] * 7 + [SMEM],
        out_specs=VMEM,
        scratch_shapes=[pltpu.VMEM((8, 5, 16, LANES), F32)],
        name="sweeps",
        compiler_params=pltpu.CompilerParams(vmem_limit_bytes=BYTES),
    )(residual, before, after, far, inv, filled, fluid, couple)


def solution(mesh):
    in_specs = (
        P(None, "stream", "cy", "cz"),
        P(None, "stream", "cy", "cz"),
        P(None, "stream", "cy", "cz"),
        P(None, None, "stream", "cy", "cz"),
        P(),
        P("stream", "cy", "cz"),
        P("stream", "cy", "cz", None, None),
        P("stream", "cy", "cz", None),
        P("stream", "cy", "cz", None),
        P("stream", "cy", "cz", None, None),
        P("stream", "cy", "cz", None, None),
    )
    out_specs = P(None, "stream", "cy", "cz")
    return jax.shard_map(
        on_device, mesh=mesh, in_specs=in_specs, out_specs=out_specs, check_vma=False
    )
```

```python
import jax
import jax.numpy as jnp
from jax import lax
from jax.experimental import pallas as pl
from jax.experimental.pallas import tpu as pltpu
from jax.sharding import PartitionSpec as P

RELAX = 0.8
LANES = 128
F32 = jnp.float32
BF16 = jnp.bfloat16
VMEM = pl.BlockSpec(memory_space=pltpu.VMEM)
SMEM = pl.BlockSpec(memory_space=pltpu.SMEM)
BYTES = 24 << 20


def ring(x, axis, steps):
    count = lax.axis_size(axis)
    return lax.ppermute(x, axis, [(i, (i + steps) % count) for i in range(count)])


def call(kernel, outs, args, specs, name):
    return pl.pallas_call(
        kernel,
        out_shape=outs,
        in_specs=specs,
        out_specs=jax.tree.map(lambda _: VMEM, outs),
        name=name,
        compiler_params=pltpu.CompilerParams(vmem_limit_bytes=BYTES),
    )(*args)


def lane_pick(rows, lane):
    return jnp.take_along_axis(rows, lane, axis=1, mode="promise_in_bounds")


def donor_kernel(
    idx_hbm, count_hbm, state_hbm, out_ref, idx_ref, count_ref, state_ref, sems
):
    moves = [
        pltpu.make_async_copy(src, dst, sems.at[n])
        for n, (src, dst) in enumerate(
            (
                (count_hbm, count_ref),
                (state_hbm, state_ref),
                (idx_hbm, idx_ref),
            )
        )
    ]
    for move in moves:
        move.start()
    for move in moves:
        move.wait()
    lanes = lax.broadcasted_iota(jnp.int32, (8, LANES), 1)
    subs = lax.broadcasted_iota(jnp.int32, (8, LANES), 0)

    def body(g, carry):
        base = pl.multiple_of(g * 8, 8)
        count = jnp.zeros((8, LANES), jnp.int32)
        for q in range(8):
            count = jnp.where(subs == q, count_ref[0, g * 8 + q], count)
        for h in range(2):
            idx = idx_ref[pl.ds(base, 8), h * LANES : (h + 1) * LANES]
            lane = idx & (LANES - 1)
            row = idx >> 7
            acc = [jnp.zeros((8, LANES), F32) for _ in range(5)]
            for r in range(32):
                hit = row == r
                for v in range(5):
                    line = state_ref[v * 32 + r : v * 32 + r + 1, :]
                    line = jnp.broadcast_to(line, (8, LANES))
                    acc[v] = jnp.where(hit, lane_pick(line, lane), acc[v])
            live = lanes + h * LANES < count
            for v in range(5):
                at = (v * 2 + h) * LANES
                out_ref[pl.ds(base, 8), 0, at : at + LANES] = jnp.where(live, acc[v], 0.0)
        return carry

    lax.fori_loop(0, 8, body, 0)


def stage_kernel(*refs):
    half = len(refs) // 2
    for src, dst in zip(refs[:half], refs[half:]):
        dst[...] = src[...]


def ghost_kernel(
    rec_ref, src_ref, w_ref, cell_ref, state_ref, f_ref, x0_ref, x1_ref, y_ref, z_ref
):
    tabs = []
    for v in range(5):
        t = rec_ref[:, 0, v * 256 : (v + 1) * 256]
        hi = t.astype(BF16)
        lo = (t - hi.astype(F32)).astype(BF16)
        tabs.append(jnp.concatenate([hi, lo], axis=1))
    tab = jnp.concatenate(tabs, axis=0)
    width = 256
    lane_ids = lax.broadcasted_iota(jnp.int32, (256, width), 0)
    row_ids = lax.broadcasted_iota(jnp.int32, (64, width), 0)
    parts = [[] for _ in range(5)]
    for j in range(1024 // width):
        at = slice(j * width, (j + 1) * width)
        acc = [jnp.zeros((8, width), F32) for _ in range(5)]
        for k in range(8):
            entry = src_ref[k : k + 1, at]
            weight = w_ref[k : k + 1, at]
            onehot = (lane_ids == (entry & 255)).astype(BF16)
            onehot = jnp.concatenate([onehot, onehot], axis=0)
            p = jnp.dot(tab, onehot, preferred_element_type=F32)
            m = jnp.where(row_ids == (entry >> 8), weight, 0.0)
            for v in range(5):
                q = p[v * 64 : (v + 1) * 64] * m
                acc[v] = acc[v] + jnp.sum(q.reshape(8, 8, width), axis=0)
        for v in range(5):
            parts[v].append(jnp.sum(acc[v], axis=0, keepdims=True))
    values = [jnp.concatenate(p, axis=1) for p in parts]

    cell = cell_ref[...]
    in_row = lax.broadcasted_iota(jnp.int32, (32, 1024), 0) == (cell >> 7)
    in_lane = lax.broadcasted_iota(jnp.int32, (LANES, 1024), 0) == (cell & (LANES - 1))
    pieces = [[], [], []]
    for v in range(5):
        x = jnp.where(in_row, values[v], 0.0)
        hi = x.astype(BF16)
        rest = x - hi.astype(F32)
        mid = rest.astype(BF16)
        pieces[0].append(hi)
        pieces[1].append(mid)
        pieces[2].append((rest - mid.astype(F32)).astype(BF16))
    left = jnp.concatenate([in_row.astype(BF16)] + pieces[0] + pieces[1] + pieces[2], axis=0)
    placed = lax.dot_general(
        left, in_lane.astype(BF16), (((1,), (1,)), ((), ())), preferred_element_type=F32
    )
    covered = placed[0:32] > 0.5
    diag = lax.broadcasted_iota(jnp.int32, (16, LANES), 0) == lax.broadcasted_iota(
        jnp.int32, (16, LANES), 1
    )
    for v in range(5):
        hi, mid, lo = (placed[32 * (1 + v + 5 * p) : 32 * (2 + v + 5 * p)] for p in range(3))
        old = state_ref[32 * v : 32 * v + 32, :]
        new = jnp.where(covered, hi + (mid + lo), old)
        f_ref[32 * v : 32 * v + 32, :] = new
        x0_ref[v] = new[0:16]
        x1_ref[v] = new[16:32]
        for x in range(2):
            plane = new[16 * x : 16 * x + 16]
            row = 2 * v + x
            y_ref[0, row : row + 1, :] = plane[0:1]
            y_ref[1, row : row + 1, :] = plane[15:16]
            for side, col in ((0, 0), (1, LANES - 1)):
                face = jnp.where(diag, plane[:, col : col + 1], 0.0)
                z_ref[side, row : row + 1, :] = jnp.sum(face, axis=0, keepdims=True)


def residual_kernel(
    f_ref, xm_ref, xp_ref, ym_ref, yp_ref, zm_ref, zp_ref, source_ref, scale_ref, fluid_ref,
    couple_ref, out_ref,
):
    s, a, b = (lax.axis_index(n) for n in ("stream", "cy", "cz"))
    ns, na, nb = (lax.axis_size(n) for n in ("stream", "cy", "cz"))
    shape = (16, LANES)
    subs = lax.broadcasted_iota(jnp.int32, shape, 0)
    lanes = lax.broadcasted_iota(jnp.int32, shape, 1)

    def column(ref, row):
        line = jnp.broadcast_to(ref[row : row + 1, :], shape)
        return jnp.concatenate(
            [lane_pick(line[0:8], subs[0:8]), lane_pick(line[8:16], subs[8:16])], axis=0
        )

    for x in range(2):
        near = [[] for _ in range(7)]
        for v in range(5):
            row = 2 * v + x
            mid = f_ref[32 * v + 16 * x : 32 * v + 16 * x + 16, :]
            other = f_ref[32 * v + 16 * (1 - x) : 32 * v + 16 * (1 - x) + 16, :]
            if x == 0:
                xm, xp = jnp.where(s > 0, xm_ref[v], 0.0), other
            else:
                xm, xp = other, jnp.where(s < ns - 1, xp_ref[v], 0.0)
            ym = jnp.where(a > 0, ym_ref[row : row + 1, :], 0.0)
            yp = jnp.where(a < na - 1, yp_ref[row : row + 1, :], 0.0)
            zm = jnp.where(b > 0, column(zm_ref, row), 0.0)
            zp = jnp.where(b < nb - 1, column(zp_ref, row), 0.0)
            near[0].append(mid)
            near[1].append(xm)
            near[2].append(xp)
            near[3].append(jnp.where(subs == 0, ym, pltpu.roll(mid, 1, 0)))
            near[4].append(jnp.where(subs == 15, yp, pltpu.roll(mid, 15, 0)))
            near[5].append(jnp.where(lanes == 0, zm, pltpu.roll(mid, 1, 1)))
            near[6].append(jnp.where(lanes == LANES - 1, zp, pltpu.roll(mid, LANES - 1, 1)))
        wet = fluid_ref[x].astype(F32)
        for i in range(5):
            image = scale_ref[i, x] * near[0][i]
            for d in range(7):
                for j in range(5):
                    image = image + couple_ref[d, i, j] * near[d][j]
            out_ref[x, i] = wet * (source_ref[i, x] - image)


def sweep_kernel(
    res_ref, prev_ref, next_ref, far_ref, inv_ref, f_ref, fluid_ref, couple_ref, out_ref, low_ref
):
    s = lax.axis_index("stream")
    count = 4
    zero = jnp.zeros((16, LANES), F32)
    prev = [zero] * 5
    for q in range(count):
        o = lax.rem(q - s + count, count)
        for x in range(2):
            t = []
            for i in range(5):
                r = jnp.where(
                    o == 0,
                    res_ref[x, i],
                    jnp.where(
                        o == 1, next_ref[x, i], jnp.where(o == 2, far_ref[x, i], prev_ref[x, i])
                    ),
                )
                for j in range(5):
                    r = r - couple_ref[1, i, j] * prev[j]
                t.append(r)
            cur = []
            for i in range(5):
                c = inv_ref[o, i, 0, x] * t[0]
                for j in range(1, 5):
                    c = c + inv_ref[o, i, j, x] * t[j]
                cur.append(c)
                low_ref[2 * q + x, i] = c
            prev = cur
    prev = [zero] * 5
    for q in reversed(range(count)):
        o = lax.rem(q - s + count, count)
        for x in (1, 0):
            t = []
            for i in range(5):
                r = couple_ref[2, i, 0] * prev[0]
                for j in range(1, 5):
                    r = r + couple_ref[2, i, j] * prev[j]
                t.append(r)
            cur = []
            for i in range(5):
                c = low_ref[2 * q + x, i]
                for j in range(5):
                    c = c - inv_ref[o, i, j, x] * t[j]
                cur.append(c)
            prev = cur

            @pl.when(o == 0)
            def _():
                wet = RELAX * fluid_ref[x].astype(F32)
                for i in range(5):
                    at = 32 * i + 16 * x
                    out_ref[i, x] = f_ref[at : at + 16, :] + wet * cur[i]


def on_device(
    state,
    source,
    diag_scale,
    diag_inverse,
    couple,
    fluid,
    donor_index,
    donor_count,
    ghost_cell,
    ghost_source,
    ghost_weight,
):
    table = state.reshape(160, LANES)
    sent = pl.pallas_call(
        donor_kernel,
        out_shape=jax.ShapeDtypeStruct((64, 1, 1280), F32),
        in_specs=[pl.BlockSpec(memory_space=pl.ANY)] * 3,
        out_specs=VMEM,
        scratch_shapes=[
            pltpu.VMEM((64, 256), jnp.int32),
            pltpu.SMEM((1, 64), jnp.int32),
            pltpu.VMEM((160, LANES), F32),
            pltpu.SemaphoreType.DMA((3,)),
        ],
        name="donor_pick",
        compiler_params=pltpu.CompilerParams(vmem_limit_bytes=60 << 20),
    )(donor_index.reshape(64, 256), donor_count.reshape(1, 64), table)
    lists = (
        ghost_source.reshape(1024, 8).T,
        ghost_weight.reshape(1024, 8).T,
        ghost_cell.reshape(1, 1024),
        table,
    )
    entries, weights, cells, table = call(
        stage_kernel,
        tuple(jax.ShapeDtypeStruct(x.shape, x.dtype) for x in lists),
        lists,
        [VMEM] * 4,
        "stage_lists",
    )
    received = lax.all_to_all(sent, ("cy", "cz"), split_axis=0, concat_axis=0, tiled=True)
    inv_prev = ring(diag_inverse, "stream", 1)
    inv_next = ring(diag_inverse, "stream", -1)
    received, inv_prev, inv_next = lax.optimization_barrier((received, inv_prev, inv_next))
    far_a, far_b = ring(inv_prev[:3], "stream", 1), ring(inv_next[3:], "stream", -1)
    plane = jax.ShapeDtypeStruct((5, 16, LANES), F32)
    faces = jax.ShapeDtypeStruct((2, 10, LANES), F32)
    filled, first, last, yface, zface = call(
        ghost_kernel,
        (jax.ShapeDtypeStruct((160, LANES), F32), plane, plane, faces, faces),
        (
            received,
            entries,
            weights,
            cells,
            table,
        ),
        [VMEM] * 5,
        "ghost_fill",
    )
    filled, first, last, yface, zface, far_a, far_b = lax.optimization_barrier(
        (filled, first, last, yface, zface, far_a, far_b)
    )
    inv = jnp.stack([diag_inverse, inv_next, jnp.concatenate([far_a, far_b]), inv_prev])
    xm, xp = ring(last, "stream", 1), ring(first, "stream", -1)
    ym, yp = ring(yface[1], "cy", 1), ring(yface[0], "cy", -1)
    zm, zp = ring(zface[1], "cz", 1), ring(zface[0], "cz", -1)
    residual = call(
        residual_kernel,
        jax.ShapeDtypeStruct((2, 5, 16, LANES), F32),
        (filled, xm, xp, ym, yp, zm, zp, source, diag_scale, fluid, couple),
        [VMEM] * 10 + [SMEM],
        "residual",
    )
    after, far, before = (ring(residual, "stream", step) for step in (-1, 2, 1))
    return pl.pallas_call(
        sweep_kernel,
        out_shape=jax.ShapeDtypeStruct((5, 2, 16, LANES), F32),
        in_specs=[VMEM] * 7 + [SMEM],
        out_specs=VMEM,
        scratch_shapes=[pltpu.VMEM((8, 5, 16, LANES), F32)],
        name="sweeps",
        compiler_params=pltpu.CompilerParams(vmem_limit_bytes=BYTES),
    )(residual, before, after, far, inv, filled, fluid, couple)


def solution(mesh):
    in_specs = (
        P(None, "stream", "cy", "cz"),
        P(None, "stream", "cy", "cz"),
        P(None, "stream", "cy", "cz"),
        P(None, None, "stream", "cy", "cz"),
        P(),
        P("stream", "cy", "cz"),
        P("stream", "cy", "cz", None, None),
        P("stream", "cy", "cz", None),
        P("stream", "cy", "cz", None),
        P("stream", "cy", "cz", None, None),
        P("stream", "cy", "cz", None, None),
    )
    out_specs = P(None, "stream", "cy", "cz")
    return jax.shard_map(
        on_device, mesh=mesh, in_specs=in_specs, out_specs=out_specs, check_vma=False
    )
```

```python
import jax
import jax.numpy as jnp
from jax import lax
from jax.experimental import pallas as pl
from jax.experimental.pallas import tpu as pltpu
from jax.sharding import PartitionSpec as P

RELAX = 0.8
LANES = 128
F32 = jnp.float32
BF16 = jnp.bfloat16
VMEM = pl.BlockSpec(memory_space=pltpu.VMEM)
SMEM = pl.BlockSpec(memory_space=pltpu.SMEM)
BYTES = 24 << 20


def ring(x, axis, steps):
    count = lax.axis_size(axis)
    return lax.ppermute(x, axis, [(i, (i + steps) % count) for i in range(count)])


def call(kernel, outs, args, specs, name):
    return pl.pallas_call(
        kernel,
        out_shape=outs,
        in_specs=specs,
        out_specs=jax.tree.map(lambda _: VMEM, outs),
        name=name,
        compiler_params=pltpu.CompilerParams(vmem_limit_bytes=BYTES),
    )(*args)


def lane_pick(rows, lane):
    return jnp.take_along_axis(rows, lane, axis=1, mode="promise_in_bounds")


def donor_kernel(
    idx_hbm, count_hbm, state_hbm, out_ref, idx_ref, count_ref, state_ref, sems
):
    moves = [
        pltpu.make_async_copy(src, dst, sems.at[n])
        for n, (src, dst) in enumerate(
            (
                (count_hbm, count_ref),
                (state_hbm, state_ref),
                (idx_hbm, idx_ref),
            )
        )
    ]
    for move in moves:
        move.start()
    for move in moves:
        move.wait()
    lanes = lax.broadcasted_iota(jnp.int32, (8, LANES), 1)
    subs = lax.broadcasted_iota(jnp.int32, (8, LANES), 0)

    def body(g, carry):
        base = pl.multiple_of(g * 8, 8)
        count = jnp.zeros((8, LANES), jnp.int32)
        for q in range(8):
            count = jnp.where(subs == q, count_ref[0, g * 8 + q], count)
        for h in range(2):
            idx = idx_ref[pl.ds(base, 8), h * LANES : (h + 1) * LANES]
            lane = idx & (LANES - 1)
            row = idx >> 7
            acc = [jnp.zeros((8, LANES), F32) for _ in range(5)]
            for r in range(32):
                hit = row == r
                for v in range(5):
                    line = state_ref[v * 32 + r : v * 32 + r + 1, :]
                    line = jnp.broadcast_to(line, (8, LANES))
                    acc[v] = jnp.where(hit, lane_pick(line, lane), acc[v])
            live = lanes + h * LANES < count
            for v in range(5):
                at = (v * 2 + h) * LANES
                out_ref[pl.ds(base, 8), 0, at : at + LANES] = jnp.where(live, acc[v], 0.0)
        return carry

    lax.fori_loop(0, 8, body, 0)


def stage_kernel(*refs):
    half = len(refs) // 2
    for src, dst in zip(refs[:half], refs[half:]):
        dst[...] = src[...]


def ghost_kernel(
    rec_ref, src_ref, w_ref, cell_ref, state_ref, f_ref, y_ref, z_ref
):
    tabs = []
    for v in range(5):
        t = rec_ref[:, 0, v * 256 : (v + 1) * 256]
        hi = t.astype(BF16)
        lo = (t - hi.astype(F32)).astype(BF16)
        tabs.append(jnp.concatenate([hi, lo], axis=1))
    tab = jnp.concatenate(tabs, axis=0)
    width = 256
    lane_ids = lax.broadcasted_iota(jnp.int32, (256, width), 0)
    row_ids = lax.broadcasted_iota(jnp.int32, (64, width), 0)
    parts = [[] for _ in range(5)]
    for j in range(1024 // width):
        at = slice(j * width, (j + 1) * width)
        acc = [jnp.zeros((8, width), F32) for _ in range(5)]
        for k in range(8):
            entry = src_ref[k : k + 1, at]
            weight = w_ref[k : k + 1, at]
            onehot = (lane_ids == (entry & 255)).astype(BF16)
            onehot = jnp.concatenate([onehot, onehot], axis=0)
            p = jnp.dot(tab, onehot, preferred_element_type=F32)
            m = jnp.where(row_ids == (entry >> 8), weight, 0.0)
            for v in range(5):
                q = p[v * 64 : (v + 1) * 64] * m
                acc[v] = acc[v] + jnp.sum(q.reshape(8, 8, width), axis=0)
        for v in range(5):
            parts[v].append(jnp.sum(acc[v], axis=0, keepdims=True))
    values = [jnp.concatenate(p, axis=1) for p in parts]

    cell = cell_ref[...]
    in_row = lax.broadcasted_iota(jnp.int32, (32, 1024), 0) == (cell >> 7)
    in_lane = lax.broadcasted_iota(jnp.int32, (LANES, 1024), 0) == (cell & (LANES - 1))
    pieces = [[], [], []]
    for v in range(5):
        x = jnp.where(in_row, values[v], 0.0)
        hi = x.astype(BF16)
        rest = x - hi.astype(F32)
        mid = rest.astype(BF16)
        pieces[0].append(hi)
        pieces[1].append(mid)
        pieces[2].append((rest - mid.astype(F32)).astype(BF16))
    left = jnp.concatenate([in_row.astype(BF16)] + pieces[0] + pieces[1] + pieces[2], axis=0)
    placed = lax.dot_general(
        left, in_lane.astype(BF16), (((1,), (1,)), ((), ())), preferred_element_type=F32
    )
    covered = placed[0:32] > 0.5
    diag = lax.broadcasted_iota(jnp.int32, (16, LANES), 0) == lax.broadcasted_iota(
        jnp.int32, (16, LANES), 1
    )
    for v in range(5):
        hi, mid, lo = (placed[32 * (1 + v + 5 * p) : 32 * (2 + v + 5 * p)] for p in range(3))
        old = state_ref[32 * v : 32 * v + 32, :]
        new = jnp.where(covered, hi + (mid + lo), old)
        f_ref[32 * v : 32 * v + 32, :] = new
        for x in range(2):
            plane = new[16 * x : 16 * x + 16]
            row = 2 * v + x
            y_ref[0, row : row + 1, :] = plane[0:1]
            y_ref[1, row : row + 1, :] = plane[15:16]
            for side, col in ((0, 0), (1, LANES - 1)):
                face = jnp.where(diag, plane[:, col : col + 1], 0.0)
                z_ref[side, row : row + 1, :] = jnp.sum(face, axis=0, keepdims=True)


def residual_kernel(
    f_ref, ym_ref, yp_ref, zm_ref, zp_ref, source_ref, scale_ref, fluid_ref,
    couple_ref, same_ref, other_ref,
):
    s, a, b = (lax.axis_index(n) for n in ("stream", "cy", "cz"))
    na, nb = (lax.axis_size(n) for n in ("cy", "cz"))
    half = lax.rem(s, 2)
    shape = (16, LANES)
    subs = lax.broadcasted_iota(jnp.int32, shape, 0)
    lanes = lax.broadcasted_iota(jnp.int32, shape, 1)

    def column(ref, row):
        line = jnp.broadcast_to(ref[row : row + 1, :], shape)
        return jnp.concatenate(
            [lane_pick(line[0:8], subs[0:8]), lane_pick(line[8:16], subs[8:16])], axis=0
        )

    for x in range(2):
        near = [[] for _ in range(7)]
        for v in range(5):
            row = 2 * v + x
            mid = f_ref[32 * v + 16 * x : 32 * v + 16 * x + 16, :]
            other = f_ref[32 * v + 16 * (1 - x) : 32 * v + 16 * (1 - x) + 16, :]
            ym = jnp.where(a > 0, ym_ref[row : row + 1, :], 0.0)
            yp = jnp.where(a < na - 1, yp_ref[row : row + 1, :], 0.0)
            zm = jnp.where(b > 0, column(zm_ref, row), 0.0)
            zp = jnp.where(b < nb - 1, column(zp_ref, row), 0.0)
            near[0].append(mid)
            near[2 - x].append(other)
            near[3].append(jnp.where(subs == 0, ym, pltpu.roll(mid, 1, 0)))
            near[4].append(jnp.where(subs == 15, yp, pltpu.roll(mid, 15, 0)))
            near[5].append(jnp.where(lanes == 0, zm, pltpu.roll(mid, 1, 1)))
            near[6].append(jnp.where(lanes == LANES - 1, zp, pltpu.roll(mid, LANES - 1, 1)))
        wet = fluid_ref[x].astype(F32)
        for i in range(5):
            image = scale_ref[i, x] * near[0][i]
            for d in (0, 2 - x, 3, 4, 5, 6):
                for j in range(5):
                    image = image + couple_ref[d, i, j] * near[d][j]
            res = wet * (source_ref[i, x] - image)
            same_ref[x, i] = jnp.where(half == 0, res[0:8], res[8:16])
            other_ref[x, i] = jnp.where(half == 0, res[8:16], res[0:8])
            same_ref[2 + x, i] = jnp.where(half == 0, near[0][i][0:8], near[0][i][8:16])
            other_ref[2 + x, i] = jnp.where(half == 0, near[0][i][8:16], near[0][i][0:8])


def sweep_kernel(
    res_ref, prev_ref, next_ref, far_ref, inv_ref, couple_ref, mine_ref, theirs_ref, low_ref
):
    s = lax.axis_index("stream")
    pair = s + 1 - 2 * lax.rem(s, 2)
    count = 4
    zero = jnp.zeros((8, LANES), F32)
    offset = [lax.rem(q - s + count, count) for q in range(count)]

    def block(q, k):
        o = offset[q]
        return [
            jnp.where(
                o == 0,
                res_ref[k, i],
                jnp.where(
                    o == 1, next_ref[k, i], jnp.where(o == 2, far_ref[k, i], prev_ref[k, i])
                ),
            )
            for i in range(5)
        ]

    prev = [zero] * 5
    for q in range(count):
        o = offset[q]
        for x in range(2):
            t = block(q, x)
            wet = inv_ref[o, 25, x]
            if x == 0 and q > 0:
                prev = [p + wet * f for p, f in zip(prev, block(q - 1, 3))]
            if x == 1 and q < count - 1:
                ahead = block(q + 1, 2)
                for i in range(5):
                    c = couple_ref[2, i, 0] * ahead[0]
                    for j in range(1, 5):
                        c = c + couple_ref[2, i, j] * ahead[j]
                    t[i] = t[i] - wet * c
            for i in range(5):
                for j in range(5):
                    t[i] = t[i] - couple_ref[1, i, j] * prev[j]
            cur = []
            for i in range(5):
                c = inv_ref[o, 5 * i, x] * t[0]
                for j in range(1, 5):
                    c = c + inv_ref[o, 5 * i + j, x] * t[j]
                cur.append(c)
                low_ref[2 * q + x, i] = c
            prev = cur
    prev = [zero] * 5
    for q in reversed(range(count)):
        o = offset[q]
        for x in (1, 0):
            t = []
            for i in range(5):
                r = couple_ref[2, i, 0] * prev[0]
                for j in range(1, 5):
                    r = r + couple_ref[2, i, j] * prev[j]
                t.append(r)
            cur = []
            for i in range(5):
                c = low_ref[2 * q + x, i]
                for j in range(5):
                    c = c - inv_ref[o, 5 * i + j, x] * t[j]
                cur.append(c)
            prev = cur
            for where, to_ref in ((s, mine_ref), (pair, theirs_ref)):

                @pl.when(where == q)
                def _():
                    for i in range(5):
                        to_ref[i, x] = cur[i]


def on_device(
    state,
    source,
    diag_scale,
    diag_inverse,
    couple,
    fluid,
    donor_index,
    donor_count,
    ghost_cell,
    ghost_source,
    ghost_weight,
):
    table = state.reshape(160, LANES)
    sent = pl.pallas_call(
        donor_kernel,
        out_shape=jax.ShapeDtypeStruct((64, 1, 1280), F32),
        in_specs=[pl.BlockSpec(memory_space=pl.ANY)] * 3,
        out_specs=VMEM,
        scratch_shapes=[
            pltpu.VMEM((64, 256), jnp.int32),
            pltpu.SMEM((1, 64), jnp.int32),
            pltpu.VMEM((160, LANES), F32),
            pltpu.SemaphoreType.DMA((3,)),
        ],
        name="donor_pick",
        compiler_params=pltpu.CompilerParams(vmem_limit_bytes=60 << 20),
    )(donor_index.reshape(64, 256), donor_count.reshape(1, 64), table)
    lists = (
        ghost_source.reshape(1024, 8).T,
        ghost_weight.reshape(1024, 8).T,
        ghost_cell.reshape(1, 1024),
        table,
    )
    entries, weights, cells, table = call(
        stage_kernel,
        tuple(jax.ShapeDtypeStruct(x.shape, x.dtype) for x in lists),
        lists,
        [VMEM] * 4,
        "stage_lists",
    )
    received = lax.all_to_all(sent, ("cy", "cz"), split_axis=0, concat_axis=0, tiled=True)
    half = lax.rem(lax.axis_index("stream"), 2)
    frozen = jnp.concatenate([diag_inverse.reshape(25, 2, 16, LANES), fluid.astype(F32)[None]])
    inv_same, inv_other = (
        lax.dynamic_slice_in_dim(frozen, 8 * h, 8, 2) for h in (half, 1 - half)
    )
    inv_prev, inv_next = ring(inv_other, "stream", 1), ring(inv_other, "stream", -1)
    inv_far = ring(inv_same, "stream", 2)
    faces = jax.ShapeDtypeStruct((2, 10, LANES), F32)
    filled, yface, zface = call(
        ghost_kernel,
        (jax.ShapeDtypeStruct((160, LANES), F32), faces, faces),
        (
            received,
            entries,
            weights,
            cells,
            table,
        ),
        [VMEM] * 5,
        "ghost_fill",
    )
    filled, yface, zface, inv_prev, inv_next, inv_far = lax.optimization_barrier(
        (filled, yface, zface, inv_prev, inv_next, inv_far)
    )
    inv = jnp.stack([inv_same, inv_next, inv_far, inv_prev])
    ym, yp = ring(yface[1], "cy", 1), ring(yface[0], "cy", -1)
    zm, zp = ring(zface[1], "cz", 1), ring(zface[0], "cz", -1)
    part = jax.ShapeDtypeStruct((4, 5, 8, LANES), F32)
    same, other = call(
        residual_kernel,
        (part, part),
        (filled, ym, yp, zm, zp, source, diag_scale, fluid, couple),
        [VMEM] * 8 + [SMEM],
        "residual",
    )
    before, after = ring(other, "stream", 1), ring(other, "stream", -1)
    far = ring(same, "stream", 2)
    part = jax.ShapeDtypeStruct((5, 2, 8, LANES), F32)
    mine, theirs = pl.pallas_call(
        sweep_kernel,
        out_shape=(part, part),
        in_specs=[VMEM] * 5 + [SMEM],
        out_specs=(VMEM, VMEM),
        scratch_shapes=[pltpu.VMEM((8, 5, 8, LANES), F32)],
        name="sweeps",
        compiler_params=pltpu.CompilerParams(vmem_limit_bytes=BYTES),
    )(same, before, after, far, inv, couple)
    swapped = lax.ppermute(
        theirs, "stream", [(i, i ^ 1) for i in range(lax.axis_size("stream"))]
    )
    first_half = jnp.where(half == 0, mine, swapped)
    second_half = jnp.where(half == 0, swapped, mine)
    upper = jnp.concatenate([first_half, second_half], axis=2)
    return filled.reshape(5, 2, 16, LANES) + RELAX * fluid.astype(F32)[None] * upper


def solution(mesh):
    in_specs = (
        P(None, "stream", "cy", "cz"),
        P(None, "stream", "cy", "cz"),
        P(None, "stream", "cy", "cz"),
        P(None, None, "stream", "cy", "cz"),
        P(),
        P("stream", "cy", "cz"),
        P("stream", "cy", "cz", None, None),
        P("stream", "cy", "cz", None),
        P("stream", "cy", "cz", None),
        P("stream", "cy", "cz", None, None),
        P("stream", "cy", "cz", None, None),
    )
    out_specs = P(None, "stream", "cy", "cz")
    return jax.shard_map(
        on_device, mesh=mesh, in_specs=in_specs, out_specs=out_specs, check_vma=False
    )
```

```python
import jax
import jax.numpy as jnp
from jax import lax
from jax.experimental import pallas as pl
from jax.experimental.pallas import tpu as pltpu
from jax.sharding import PartitionSpec as P

RELAX = 0.8
LANES = 128
F32 = jnp.float32
BF16 = jnp.bfloat16
VMEM = pl.BlockSpec(memory_space=pltpu.VMEM)
SMEM = pl.BlockSpec(memory_space=pltpu.SMEM)
BYTES = 24 << 20


def ring(x, axis, steps):
    count = lax.axis_size(axis)
    return lax.ppermute(x, axis, [(i, (i + steps) % count) for i in range(count)])


def call(kernel, outs, args, specs, name):
    return pl.pallas_call(
        kernel,
        out_shape=outs,
        in_specs=specs,
        out_specs=jax.tree.map(lambda _: VMEM, outs),
        name=name,
        compiler_params=pltpu.CompilerParams(vmem_limit_bytes=BYTES),
    )(*args)


def lane_pick(rows, lane):
    return jnp.take_along_axis(rows, lane, axis=1, mode="promise_in_bounds")


def donor_kernel(
    idx_hbm, count_hbm, state_hbm, out_ref, idx_ref, count_ref, state_ref, tab_ref, sems
):
    moves = [
        pltpu.make_async_copy(src, dst, sems.at[n])
        for n, (src, dst) in enumerate(
            ((count_hbm, count_ref), (state_hbm, state_ref), (idx_hbm, idx_ref))
        )
    ]
    for move in moves:
        move.start()
    for move in moves:
        move.wait()
    lanes = lax.broadcasted_iota(jnp.int32, (8, LANES), 1)
    subs = lax.broadcasted_iota(jnp.int32, (8, LANES), 0)
    lane_ids = lax.broadcasted_iota(jnp.int32, (LANES, 256), 0)
    slots = lax.broadcasted_iota(jnp.int32, (1, 256), 1)
    tab_ref[...] = jnp.zeros_like(tab_ref)
    for v in range(5):
        tab_ref[pl.ds(v, 32, stride=8), :] = state_ref[v * 32 : v * 32 + 32, :]
    whole = tab_ref[...]
    hi = whole.astype(BF16)
    tab = jnp.concatenate([hi, (whole - hi.astype(F32)).astype(BF16)], axis=1)
    for g in range(4):
        count = jnp.zeros((8, LANES), jnp.int32)
        for q in range(8):
            count = jnp.where(subs == q, count_ref[0, g * 8 + q], count)
        for h in range(2):
            idx = idx_ref[g * 8 : g * 8 + 8, h * LANES : (h + 1) * LANES]
            lane = idx & (LANES - 1)
            row = idx >> 7
            acc = [jnp.zeros((8, LANES), F32) for _ in range(5)]
            for r in range(32):
                hit = row == r
                for v in range(5):
                    line = state_ref[v * 32 + r : v * 32 + r + 1, :]
                    line = jnp.broadcast_to(line, (8, LANES))
                    acc[v] = jnp.where(hit, lane_pick(line, lane), acc[v])
            live = lanes + h * LANES < count
            for v in range(5):
                at = pl.ds(g * 80 + v * 2 + h, 8, stride=10)
                out_ref[at, :] = jnp.where(live, acc[v], 0.0)
        for d in range(32 + g * 8, 40 + g * 8):
            idx = idx_ref[d : d + 1, :]
            onehot = (lane_ids == (idx & (LANES - 1))).astype(BF16)
            onehot = jnp.concatenate([onehot, onehot], axis=0)
            p = jnp.dot(tab, onehot, preferred_element_type=F32)
            row = jnp.where(slots < count_ref[0, d], idx >> 7, -1)
            row = jnp.broadcast_to(row, (8, 256))
            acc = jnp.zeros((8, 256), F32)
            for r in range(32):
                acc = jnp.where(row == r, p[r * 8 : r * 8 + 8], acc)
            for h in range(2):
                at = pl.ds(d * 10 + h, 5, stride=2)
                out_ref[at, :] = acc[0:5, h * LANES : (h + 1) * LANES]


def stage_kernel(*refs):
    half = len(refs) // 2
    for src, dst in zip(refs[:half], refs[half:]):
        dst[...] = src[...]


def ghost_kernel(
    rec_ref, src_ref, w_ref, cell_ref, state_ref, f_ref, y_ref, z_ref
):
    his, los = [], []
    for v in range(5):
        t = jnp.concatenate(
            [rec_ref[pl.ds(v * 2 + h, 64, stride=10), :] for h in range(2)], axis=1
        )
        hi = t.astype(BF16)
        his.append(hi)
        los.append((t - hi.astype(F32)).astype(BF16))
    tab = jnp.concatenate(his + los, axis=0)
    width = 256
    lane_ids = lax.broadcasted_iota(jnp.int32, (256, width), 0)
    row_ids = lax.broadcasted_iota(jnp.int32, (64, width), 0)
    parts = [[] for _ in range(5)]
    for j in range(1024 // width):
        at = slice(j * width, (j + 1) * width)
        acc = [jnp.zeros((8, width), F32) for _ in range(5)]
        for k in range(8):
            entry = src_ref[k : k + 1, at]
            weight = w_ref[k : k + 1, at]
            onehot = (lane_ids == (entry & 255)).astype(BF16)
            p = jnp.dot(tab, onehot, preferred_element_type=F32)
            m = jnp.where(row_ids == (entry >> 8), weight, 0.0)
            for v in range(5):
                q = (p[64 * v : 64 * v + 64] + p[320 + 64 * v : 384 + 64 * v]) * m
                acc[v] = acc[v] + jnp.sum(q.reshape(8, 8, width), axis=0)
        for v in range(5):
            parts[v].append(jnp.sum(acc[v], axis=0, keepdims=True))
    values = [jnp.concatenate(p, axis=1) for p in parts]

    cell = cell_ref[...]
    in_row = lax.broadcasted_iota(jnp.int32, (32, 1024), 0) == (cell >> 7)
    in_lane = lax.broadcasted_iota(jnp.int32, (LANES, 1024), 0) == (cell & (LANES - 1))
    pieces = [[], [], []]
    for v in range(5):
        x = jnp.where(in_row, values[v], 0.0)
        hi = x.astype(BF16)
        rest = x - hi.astype(F32)
        mid = rest.astype(BF16)
        pieces[0].append(hi)
        pieces[1].append(mid)
        pieces[2].append((rest - mid.astype(F32)).astype(BF16))
    left = jnp.concatenate([in_row.astype(BF16)] + pieces[0] + pieces[1] + pieces[2], axis=0)
    placed = lax.dot_general(
        left, in_lane.astype(BF16), (((1,), (1,)), ((), ())), preferred_element_type=F32
    )
    covered = placed[0:32] > 0.5
    diag = lax.broadcasted_iota(jnp.int32, (16, LANES), 0) == lax.broadcasted_iota(
        jnp.int32, (16, LANES), 1
    )
    for v in range(5):
        hi, mid, lo = (placed[32 * (1 + v + 5 * p) : 32 * (2 + v + 5 * p)] for p in range(3))
        old = state_ref[32 * v : 32 * v + 32, :]
        new = jnp.where(covered, hi + (mid + lo), old)
        f_ref[32 * v : 32 * v + 32, :] = new
        for x in range(2):
            plane = new[16 * x : 16 * x + 16]
            row = 2 * v + x
            y_ref[0, row : row + 1, :] = plane[0:1]
            y_ref[1, row : row + 1, :] = plane[15:16]
            for side, col in ((0, 0), (1, LANES - 1)):
                face = jnp.where(diag, plane[:, col : col + 1], 0.0)
                z_ref[side, row : row + 1, :] = jnp.sum(face, axis=0, keepdims=True)


def residual_kernel(
    f_ref, ym_ref, yp_ref, zm_ref, zp_ref, source_ref, scale_ref, fluid_ref,
    couple_ref, same_ref, other_ref,
):
    s, a, b = (lax.axis_index(n) for n in ("stream", "cy", "cz"))
    na, nb = (lax.axis_size(n) for n in ("cy", "cz"))
    half = lax.rem(s, 2)
    shape = (16, LANES)
    subs = lax.broadcasted_iota(jnp.int32, shape, 0)
    lanes = lax.broadcasted_iota(jnp.int32, shape, 1)

    def column(ref, row):
        line = jnp.broadcast_to(ref[row : row + 1, :], shape)
        return jnp.concatenate(
            [lane_pick(line[0:8], subs[0:8]), lane_pick(line[8:16], subs[8:16])], axis=0
        )

    for x in range(2):
        near = [[] for _ in range(7)]
        for v in range(5):
            row = 2 * v + x
            mid = f_ref[32 * v + 16 * x : 32 * v + 16 * x + 16, :]
            other = f_ref[32 * v + 16 * (1 - x) : 32 * v + 16 * (1 - x) + 16, :]
            ym = jnp.where(a > 0, ym_ref[row : row + 1, :], 0.0)
            yp = jnp.where(a < na - 1, yp_ref[row : row + 1, :], 0.0)
            zm = jnp.where(b > 0, column(zm_ref, row), 0.0)
            zp = jnp.where(b < nb - 1, column(zp_ref, row), 0.0)
            near[0].append(mid)
            near[2 - x].append(other)
            near[3].append(jnp.where(subs == 0, ym, pltpu.roll(mid, 1, 0)))
            near[4].append(jnp.where(subs == 15, yp, pltpu.roll(mid, 15, 0)))
            near[5].append(jnp.where(lanes == 0, zm, pltpu.roll(mid, 1, 1)))
            near[6].append(jnp.where(lanes == LANES - 1, zp, pltpu.roll(mid, LANES - 1, 1)))
        wet = fluid_ref[x].astype(F32)
        for i in range(5):
            image = scale_ref[i, x] * near[0][i]
            for d in (0, 2 - x, 3, 4, 5, 6):
                for j in range(5):
                    image = image + couple_ref[d, i, j] * near[d][j]
            res = wet * (source_ref[i, x] - image)
            same_ref[x, i] = jnp.where(half == 0, res[0:8], res[8:16])
            other_ref[x, i] = jnp.where(half == 0, res[8:16], res[0:8])
            same_ref[2 + x, i] = jnp.where(half == 0, near[0][i][0:8], near[0][i][8:16])
            other_ref[2 + x, i] = jnp.where(half == 0, near[0][i][8:16], near[0][i][0:8])


def sweep_kernel(
    res_ref, prev_ref, next_ref, far_ref, inv_ref, couple_ref, mine_ref, theirs_ref, low_ref
):
    s = lax.axis_index("stream")
    pair = s + 1 - 2 * lax.rem(s, 2)
    count = 4
    zero = jnp.zeros((8, LANES), F32)
    offset = [lax.rem(q - s + count, count) for q in range(count)]

    def block(q, k):
        o = offset[q]
        return [
            jnp.where(
                o == 0,
                res_ref[k, i],
                jnp.where(
                    o == 1, next_ref[k, i], jnp.where(o == 2, far_ref[k, i], prev_ref[k, i])
                ),
            )
            for i in range(5)
        ]

    prev = [zero] * 5
    for q in range(count):
        o = offset[q]
        for x in range(2):
            t = block(q, x)
            wet = inv_ref[o, 25, x]
            if x == 0 and q > 0:
                prev = [p + wet * f for p, f in zip(prev, block(q - 1, 3))]
            if x == 1 and q < count - 1:
                ahead = block(q + 1, 2)
                for i in range(5):
                    c = couple_ref[2, i, 0] * ahead[0]
                    for j in range(1, 5):
                        c = c + couple_ref[2, i, j] * ahead[j]
                    t[i] = t[i] - wet * c
            for i in range(5):
                for j in range(5):
                    t[i] = t[i] - couple_ref[1, i, j] * prev[j]
            cur = []
            for i in range(5):
                c = inv_ref[o, 5 * i, x] * t[0]
                for j in range(1, 5):
                    c = c + inv_ref[o, 5 * i + j, x] * t[j]
                cur.append(c)
                low_ref[2 * q + x, i] = c
            prev = cur
    prev = [zero] * 5
    for q in reversed(range(count)):
        o = offset[q]
        for x in (1, 0):
            t = []
            for i in range(5):
                r = couple_ref[2, i, 0] * prev[0]
                for j in range(1, 5):
                    r = r + couple_ref[2, i, j] * prev[j]
                t.append(r)
            cur = []
            for i in range(5):
                c = low_ref[2 * q + x, i]
                for j in range(5):
                    c = c - inv_ref[o, 5 * i + j, x] * t[j]
                cur.append(c)
            prev = cur
            for where, to_ref in ((s, mine_ref), (pair, theirs_ref)):

                @pl.when(where == q)
                def _():
                    for i in range(5):
                        to_ref[i, x] = cur[i]


def on_device(
    state,
    source,
    diag_scale,
    diag_inverse,
    couple,
    fluid,
    donor_index,
    donor_count,
    ghost_cell,
    ghost_source,
    ghost_weight,
):
    table = state.reshape(160, LANES)
    sent = pl.pallas_call(
        donor_kernel,
        out_shape=jax.ShapeDtypeStruct((640, LANES), F32),
        in_specs=[pl.BlockSpec(memory_space=pl.ANY)] * 3,
        out_specs=VMEM,
        scratch_shapes=[
            pltpu.VMEM((64, 256), jnp.int32),
            pltpu.SMEM((1, 64), jnp.int32),
            pltpu.VMEM((160, LANES), F32),
            pltpu.VMEM((256, LANES), F32),
            pltpu.SemaphoreType.DMA((3,)),
        ],
        name="donor_pick",
        compiler_params=pltpu.CompilerParams(vmem_limit_bytes=60 << 20),
    )(donor_index.reshape(64, 256), donor_count.reshape(1, 64), table)
    lists = (
        ghost_source.reshape(1024, 8).T,
        ghost_weight.reshape(1024, 8).T,
        ghost_cell.reshape(1, 1024),
        table,
    )
    entries, weights, cells, table = call(
        stage_kernel,
        tuple(jax.ShapeDtypeStruct(x.shape, x.dtype) for x in lists),
        lists,
        [VMEM] * 4,
        "stage_lists",
    )
    sent = sent.reshape(64, 1, 1280)
    received = lax.all_to_all(sent, ("cy", "cz"), split_axis=0, concat_axis=0, tiled=True)
    half = lax.rem(lax.axis_index("stream"), 2)
    frozen = jnp.concatenate([diag_inverse.reshape(25, 2, 16, LANES), fluid.astype(F32)[None]])
    inv_same, inv_other = (
        lax.dynamic_slice_in_dim(frozen, 8 * h, 8, 2) for h in (half, 1 - half)
    )
    inv_prev, inv_next = ring(inv_other, "stream", 1), ring(inv_other, "stream", -1)
    inv_far = ring(inv_same, "stream", 2)
    faces = jax.ShapeDtypeStruct((2, 10, LANES), F32)
    filled, yface, zface = call(
        ghost_kernel,
        (jax.ShapeDtypeStruct((160, LANES), F32), faces, faces),
        (
            received.reshape(640, LANES),
            entries,
            weights,
            cells,
            table,
        ),
        [VMEM] * 5,
        "ghost_fill",
    )
    filled, yface, zface, inv_prev, inv_next, inv_far = lax.optimization_barrier(
        (filled, yface, zface, inv_prev, inv_next, inv_far)
    )
    inv = jnp.stack([inv_same, inv_next, inv_far, inv_prev])
    ym, yp = ring(yface[1], "cy", 1), ring(yface[0], "cy", -1)
    zm, zp = ring(zface[1], "cz", 1), ring(zface[0], "cz", -1)
    part = jax.ShapeDtypeStruct((4, 5, 8, LANES), F32)
    same, other = call(
        residual_kernel,
        (part, part),
        (filled, ym, yp, zm, zp, source, diag_scale, fluid, couple),
        [VMEM] * 8 + [SMEM],
        "residual",
    )
    before, after = ring(other, "stream", 1), ring(other, "stream", -1)
    far = ring(same, "stream", 2)
    part = jax.ShapeDtypeStruct((5, 2, 8, LANES), F32)
    mine, theirs = pl.pallas_call(
        sweep_kernel,
        out_shape=(part, part),
        in_specs=[VMEM] * 5 + [SMEM],
        out_specs=(VMEM, VMEM),
        scratch_shapes=[pltpu.VMEM((8, 5, 8, LANES), F32)],
        name="sweeps",
        compiler_params=pltpu.CompilerParams(vmem_limit_bytes=BYTES),
    )(same, before, after, far, inv, couple)
    swapped = lax.ppermute(
        theirs, "stream", [(i, i ^ 1) for i in range(lax.axis_size("stream"))]
    )
    first_half = jnp.where(half == 0, mine, swapped)
    second_half = jnp.where(half == 0, swapped, mine)
    upper = jnp.concatenate([first_half, second_half], axis=2)
    return filled.reshape(5, 2, 16, LANES) + RELAX * fluid.astype(F32)[None] * upper


def solution(mesh):
    in_specs = (
        P(None, "stream", "cy", "cz"),
        P(None, "stream", "cy", "cz"),
        P(None, "stream", "cy", "cz"),
        P(None, None, "stream", "cy", "cz"),
        P(),
        P("stream", "cy", "cz"),
        P("stream", "cy", "cz", None, None),
        P("stream", "cy", "cz", None),
        P("stream", "cy", "cz", None),
        P("stream", "cy", "cz", None, None),
        P("stream", "cy", "cz", None, None),
    )
    out_specs = P(None, "stream", "cy", "cz")
    return jax.shard_map(
        on_device, mesh=mesh, in_specs=in_specs, out_specs=out_specs, check_vma=False
    )
```

```python
import jax
import jax.numpy as jnp
from jax import lax
from jax.experimental import pallas as pl
from jax.experimental.pallas import tpu as pltpu
from jax.sharding import PartitionSpec as P

RELAX = 0.8
LANES = 128
F32 = jnp.float32
BF16 = jnp.bfloat16
VMEM = pl.BlockSpec(memory_space=pltpu.VMEM)
SMEM = pl.BlockSpec(memory_space=pltpu.SMEM)
BYTES = 24 << 20


def ring(x, axis, steps):
    count = lax.axis_size(axis)
    return lax.ppermute(x, axis, [(i, (i + steps) % count) for i in range(count)])


def call(kernel, outs, args, specs, name):
    return pl.pallas_call(
        kernel,
        out_shape=outs,
        in_specs=specs,
        out_specs=jax.tree.map(lambda _: VMEM, outs),
        name=name,
        compiler_params=pltpu.CompilerParams(vmem_limit_bytes=BYTES),
    )(*args)


def lane_pick(rows, lane):
    return jnp.take_along_axis(rows, lane, axis=1, mode="promise_in_bounds")


def donor_kernel(
    idx_hbm, count_hbm, state_hbm, out_ref, idx_ref, count_ref, state_ref, tab_ref, sems
):
    moves = [
        pltpu.make_async_copy(src, dst, sems.at[n])
        for n, (src, dst) in enumerate(
            ((count_hbm, count_ref), (state_hbm, state_ref), (idx_hbm, idx_ref))
        )
    ]
    for move in moves:
        move.start()
    for move in moves:
        move.wait()
    lanes = lax.broadcasted_iota(jnp.int32, (8, LANES), 1)
    subs = lax.broadcasted_iota(jnp.int32, (8, LANES), 0)
    lane_ids = lax.broadcasted_iota(jnp.int32, (LANES, 256), 0)
    slots = lax.broadcasted_iota(jnp.int32, (1, 256), 1)
    tab_ref[...] = jnp.zeros_like(tab_ref)
    for v in range(5):
        tab_ref[pl.ds(v, 32, stride=8), :] = state_ref[v * 32 : v * 32 + 32, :]
    whole = tab_ref[...]
    hi = whole.astype(BF16)
    tab = jnp.concatenate([hi, (whole - hi.astype(F32)).astype(BF16)], axis=1)
    for g in range(4):
        count = jnp.zeros((8, LANES), jnp.int32)
        for q in range(8):
            count = jnp.where(subs == q, count_ref[0, g * 8 + q], count)
        for h in range(2):
            idx = idx_ref[g * 8 : g * 8 + 8, h * LANES : (h + 1) * LANES]
            lane = idx & (LANES - 1)
            row = idx >> 7
            acc = [jnp.zeros((8, LANES), F32) for _ in range(5)]
            for r in range(32):
                hit = row == r
                for v in range(5):
                    line = state_ref[v * 32 + r : v * 32 + r + 1, :]
                    line = jnp.broadcast_to(line, (8, LANES))
                    acc[v] = jnp.where(hit, lane_pick(line, lane), acc[v])
            live = lanes + h * LANES < count
            for v in range(5):
                at = pl.ds(g * 80 + v * 2 + h, 8, stride=10)
                out_ref[at, :] = jnp.where(live, acc[v], 0.0)
        for d in range(32 + g * 8, 40 + g * 8):
            idx = idx_ref[d : d + 1, :]
            onehot = (lane_ids == (idx & (LANES - 1))).astype(BF16)
            onehot = jnp.concatenate([onehot, onehot], axis=0)
            p = jnp.dot(tab, onehot, preferred_element_type=F32)
            row = jnp.where(slots < count_ref[0, d], idx >> 7, -1)
            row = jnp.broadcast_to(row, (8, 256))
            acc = jnp.zeros((8, 256), F32)
            for r in range(32):
                acc = jnp.where(row == r, p[r * 8 : r * 8 + 8], acc)
            for h in range(2):
                at = pl.ds(d * 10 + h, 5, stride=2)
                out_ref[at, :] = acc[0:5, h * LANES : (h + 1) * LANES]


def coef(ref, d, i, j):
    return ref[25 * d + 5 * i + j : 25 * d + 5 * i + j + 1, :]


def stage_kernel(*refs):
    for src, dst in zip(refs[:4], refs[5:9]):
        dst[...] = src[...]
    couple_ref, coef_ref = refs[4], refs[9]
    for d in range(7):
        for i in range(5):
            for j in range(5):
                at = 25 * d + 5 * i + j
                coef_ref[at : at + 1, :] = jnp.full((1, LANES), couple_ref[d, i, j], F32)


def ghost_kernel(
    rec_ref, src_ref, w_ref, cell_ref, state_ref, f_ref, y_ref, z_ref
):
    his, los = [], []
    for v in range(5):
        t = jnp.concatenate(
            [rec_ref[pl.ds(v * 2 + h, 64, stride=10), :] for h in range(2)], axis=1
        )
        hi = t.astype(BF16)
        his.append(hi)
        los.append((t - hi.astype(F32)).astype(BF16))
    tab = jnp.concatenate(his + los, axis=0)
    width = 256
    lane_ids = lax.broadcasted_iota(jnp.int32, (256, width), 0)
    row_ids = lax.broadcasted_iota(jnp.int32, (64, width), 0)
    parts = [[] for _ in range(5)]
    for j in range(1024 // width):
        at = slice(j * width, (j + 1) * width)
        acc = [jnp.zeros((8, width), F32) for _ in range(5)]
        for k in range(8):
            entry = src_ref[k : k + 1, at]
            weight = w_ref[k : k + 1, at]
            onehot = (lane_ids == (entry & 255)).astype(BF16)
            p = jnp.dot(tab, onehot, preferred_element_type=F32)
            m = jnp.where(row_ids == (entry >> 8), weight, 0.0)
            for v in range(5):
                q = (p[64 * v : 64 * v + 64] + p[320 + 64 * v : 384 + 64 * v]) * m
                acc[v] = acc[v] + jnp.sum(q.reshape(8, 8, width), axis=0)
        for v in range(5):
            parts[v].append(jnp.sum(acc[v], axis=0, keepdims=True))
    values = [jnp.concatenate(p, axis=1) for p in parts]

    cell = cell_ref[...]
    in_row = lax.broadcasted_iota(jnp.int32, (32, 1024), 0) == (cell >> 7)
    in_lane = lax.broadcasted_iota(jnp.int32, (LANES, 1024), 0) == (cell & (LANES - 1))
    pieces = [[], [], []]
    for v in range(5):
        x = jnp.where(in_row, values[v], 0.0)
        hi = x.astype(BF16)
        rest = x - hi.astype(F32)
        mid = rest.astype(BF16)
        pieces[0].append(hi)
        pieces[1].append(mid)
        pieces[2].append((rest - mid.astype(F32)).astype(BF16))
    left = jnp.concatenate([in_row.astype(BF16)] + pieces[0] + pieces[1] + pieces[2], axis=0)
    placed = lax.dot_general(
        left, in_lane.astype(BF16), (((1,), (1,)), ((), ())), preferred_element_type=F32
    )
    covered = placed[0:32] > 0.5
    diag = lax.broadcasted_iota(jnp.int32, (16, LANES), 0) == lax.broadcasted_iota(
        jnp.int32, (16, LANES), 1
    )
    for v in range(5):
        hi, mid, lo = (placed[32 * (1 + v + 5 * p) : 32 * (2 + v + 5 * p)] for p in range(3))
        old = state_ref[32 * v : 32 * v + 32, :]
        new = jnp.where(covered, hi + (mid + lo), old)
        f_ref[32 * v : 32 * v + 32, :] = new
        for x in range(2):
            plane = new[16 * x : 16 * x + 16]
            row = 2 * v + x
            y_ref[0, row : row + 1, :] = plane[0:1]
            y_ref[1, row : row + 1, :] = plane[15:16]
            for side, col in ((0, 0), (1, LANES - 1)):
                face = jnp.where(diag, plane[:, col : col + 1], 0.0)
                z_ref[side, row : row + 1, :] = jnp.sum(face, axis=0, keepdims=True)


def interior_kernel(f_ref, source_ref, scale_ref, couple_ref, out_ref):
    shape = (16, LANES)
    subs = lax.broadcasted_iota(jnp.int32, shape, 0)
    lanes = lax.broadcasted_iota(jnp.int32, shape, 1)
    for x in range(2):
        near = [[] for _ in range(6)]
        for v in range(5):
            mid = f_ref[32 * v + 16 * x : 32 * v + 16 * x + 16, :]
            near[0].append(mid)
            near[1].append(f_ref[32 * v + 16 * (1 - x) : 32 * v + 16 * (1 - x) + 16, :])
            near[2].append(jnp.where(subs == 0, 0.0, pltpu.roll(mid, 1, 0)))
            near[3].append(jnp.where(subs == 15, 0.0, pltpu.roll(mid, 15, 0)))
            near[4].append(jnp.where(lanes == 0, 0.0, pltpu.roll(mid, 1, 1)))
            near[5].append(jnp.where(lanes == LANES - 1, 0.0, pltpu.roll(mid, LANES - 1, 1)))
        for i in range(5):
            image = scale_ref[i, x] * near[0][i]
            for n, d in enumerate((0, 2 - x, 3, 4, 5, 6)):
                for j in range(5):
                    image = image + coef(couple_ref, d, i, j) * near[n][j]
            out_ref[x, i] = source_ref[i, x] - image


def residual_kernel(
    part_ref, f_ref, ym_ref, yp_ref, zm_ref, zp_ref, fluid_ref, couple_ref, same_ref, other_ref
):
    s, a, b = (lax.axis_index(n) for n in ("stream", "cy", "cz"))
    na, nb = (lax.axis_size(n) for n in ("cy", "cz"))
    half = lax.rem(s, 2)
    subs = lax.broadcasted_iota(jnp.int32, (8, LANES), 0)
    lanes = lax.broadcasted_iota(jnp.int32, (8, LANES), 1)

    def applied(d, ref, inside):
        rows = [jnp.where(inside, ref[2 * j : 2 * j + 2, :], 0.0) for j in range(5)]
        out = []
        for i in range(5):
            c = coef(couple_ref, d, i, 0) * rows[0]
            for j in range(1, 5):
                c = c + coef(couple_ref, d, i, j) * rows[j]
            out.append(c)
        return out

    ym, yp = applied(3, ym_ref, a > 0), applied(4, yp_ref, a < na - 1)
    zm, zp = applied(5, zm_ref, b > 0), applied(6, zp_ref, b < nb - 1)
    for x in range(2):
        for i in range(5):
            tiles, filled = [], []
            for t in range(2):
                r = part_ref[x, i, 8 * t : 8 * t + 8, :]
                edge = (ym if t == 0 else yp)[i][x : x + 1]
                r = r - jnp.where(subs == 7 * t, edge, 0.0)
                left, right = (
                    lane_pick(jnp.broadcast_to(z[i][x : x + 1], (8, LANES)), subs + 8 * t)
                    for z in (zm, zp)
                )
                r = r - jnp.where(lanes == 0, left, jnp.where(lanes == LANES - 1, right, 0.0))
                tiles.append(fluid_ref[x, 8 * t : 8 * t + 8, :].astype(F32) * r)
                at = 32 * i + 16 * x + 8 * t
                filled.append(f_ref[at : at + 8, :])
            for k, (first, second) in ((x, tiles), (2 + x, filled)):
                same_ref[k, i] = jnp.where(half == 0, first, second)
                other_ref[k, i] = jnp.where(half == 0, second, first)


def sweep_kernel(
    res_ref, prev_ref, next_ref, far_ref, inv_ref, couple_ref, mine_ref, theirs_ref, low_ref
):
    s = lax.axis_index("stream")
    pair = s + 1 - 2 * lax.rem(s, 2)
    count = 4
    zero = jnp.zeros((8, LANES), F32)
    offset = [lax.rem(q - s + count, count) for q in range(count)]

    def block(q, k):
        o = offset[q]
        return [
            jnp.where(
                o == 0,
                res_ref[k, i],
                jnp.where(
                    o == 1, next_ref[k, i], jnp.where(o == 2, far_ref[k, i], prev_ref[k, i])
                ),
            )
            for i in range(5)
        ]

    prev = [zero] * 5
    for q in range(count):
        o = offset[q]
        for x in range(2):
            t = block(q, x)
            wet = inv_ref[o, 25, x]
            if x == 0 and q > 0:
                prev = [p + wet * f for p, f in zip(prev, block(q - 1, 3))]
            if x == 1 and q < count - 1:
                ahead = block(q + 1, 2)
                for i in range(5):
                    c = coef(couple_ref, 2, i, 0) * ahead[0]
                    for j in range(1, 5):
                        c = c + coef(couple_ref, 2, i, j) * ahead[j]
                    t[i] = t[i] - wet * c
            for i in range(5):
                for j in range(5):
                    t[i] = t[i] - coef(couple_ref, 1, i, j) * prev[j]
            cur = []
            for i in range(5):
                c = inv_ref[o, 5 * i, x] * t[0]
                for j in range(1, 5):
                    c = c + inv_ref[o, 5 * i + j, x] * t[j]
                cur.append(c)
                low_ref[2 * q + x, i] = c
            prev = cur
    prev = [zero] * 5
    for q in reversed(range(count)):
        o = offset[q]
        for x in (1, 0):
            t = []
            for i in range(5):
                r = coef(couple_ref, 2, i, 0) * prev[0]
                for j in range(1, 5):
                    r = r + coef(couple_ref, 2, i, j) * prev[j]
                t.append(r)
            cur = []
            for i in range(5):
                c = low_ref[2 * q + x, i]
                for j in range(5):
                    c = c - inv_ref[o, 5 * i + j, x] * t[j]
                cur.append(c)
            prev = cur
            for where, to_ref in ((s, mine_ref), (pair, theirs_ref)):

                @pl.when(where == q)
                def _():
                    for i in range(5):
                        to_ref[i, x] = cur[i]


def on_device(
    state,
    source,
    diag_scale,
    diag_inverse,
    couple,
    fluid,
    donor_index,
    donor_count,
    ghost_cell,
    ghost_source,
    ghost_weight,
):
    table = state.reshape(160, LANES)
    sent = pl.pallas_call(
        donor_kernel,
        out_shape=jax.ShapeDtypeStruct((640, LANES), F32),
        in_specs=[pl.BlockSpec(memory_space=pl.ANY)] * 3,
        out_specs=VMEM,
        scratch_shapes=[
            pltpu.VMEM((64, 256), jnp.int32),
            pltpu.SMEM((1, 64), jnp.int32),
            pltpu.VMEM((160, LANES), F32),
            pltpu.VMEM((256, LANES), F32),
            pltpu.SemaphoreType.DMA((3,)),
        ],
        name="donor_pick",
        compiler_params=pltpu.CompilerParams(vmem_limit_bytes=60 << 20),
    )(donor_index.reshape(64, 256), donor_count.reshape(1, 64), table)
    lists = (
        ghost_source.reshape(1024, 8).T,
        ghost_weight.reshape(1024, 8).T,
        ghost_cell.reshape(1, 1024),
        table,
    )
    entries, weights, cells, table, coefs = call(
        stage_kernel,
        tuple(jax.ShapeDtypeStruct(x.shape, x.dtype) for x in lists)
        + (jax.ShapeDtypeStruct((175, LANES), F32),),
        lists + (couple,),
        [VMEM] * 4 + [SMEM],
        "stage_lists",
    )
    sent = sent.reshape(64, 1, 1280)
    received = lax.all_to_all(sent, ("cy", "cz"), split_axis=0, concat_axis=0, tiled=True)
    half = lax.rem(lax.axis_index("stream"), 2)
    frozen = jnp.concatenate([diag_inverse.reshape(25, 2, 16, LANES), fluid.astype(F32)[None]])
    inv_same, inv_other = (
        lax.dynamic_slice_in_dim(frozen, 8 * h, 8, 2) for h in (half, 1 - half)
    )
    inv_prev, inv_next = ring(inv_other, "stream", 1), ring(inv_other, "stream", -1)
    inv_far = ring(inv_same, "stream", 2)
    faces = jax.ShapeDtypeStruct((2, 10, LANES), F32)
    filled, yface, zface = call(
        ghost_kernel,
        (jax.ShapeDtypeStruct((160, LANES), F32), faces, faces),
        (
            received.reshape(640, LANES),
            entries,
            weights,
            cells,
            table,
        ),
        [VMEM] * 5,
        "ghost_fill",
    )
    filled, yface, zface, inv_prev, inv_next, inv_far = lax.optimization_barrier(
        (filled, yface, zface, inv_prev, inv_next, inv_far)
    )
    inv = jnp.stack([inv_same, inv_next, inv_far, inv_prev])
    ym, yp = ring(yface[1], "cy", 1), ring(yface[0], "cy", -1)
    zm, zp = ring(zface[1], "cz", 1), ring(zface[0], "cz", -1)
    part = jax.ShapeDtypeStruct((4, 5, 8, LANES), F32)
    inside = call(
        interior_kernel,
        jax.ShapeDtypeStruct((2, 5, 16, LANES), F32),
        (filled, source, diag_scale, coefs),
        [VMEM] * 4,
        "interior",
    )
    same, other = call(
        residual_kernel,
        (part, part),
        (inside, filled, ym, yp, zm, zp, fluid, coefs),
        [VMEM] * 7 + [VMEM],
        "residual",
    )
    before, after = ring(other, "stream", 1), ring(other, "stream", -1)
    far = ring(same, "stream", 2)
    part = jax.ShapeDtypeStruct((5, 2, 8, LANES), F32)
    mine, theirs = pl.pallas_call(
        sweep_kernel,
        out_shape=(part, part),
        in_specs=[VMEM] * 6,
        out_specs=(VMEM, VMEM),
        scratch_shapes=[pltpu.VMEM((8, 5, 8, LANES), F32)],
        name="sweeps",
        compiler_params=pltpu.CompilerParams(vmem_limit_bytes=BYTES),
    )(same, before, after, far, inv, coefs)
    swapped = lax.ppermute(
        theirs, "stream", [(i, i ^ 1) for i in range(lax.axis_size("stream"))]
    )
    first_half = jnp.where(half == 0, mine, swapped)
    second_half = jnp.where(half == 0, swapped, mine)
    upper = jnp.concatenate([first_half, second_half], axis=2)
    return filled.reshape(5, 2, 16, LANES) + RELAX * fluid.astype(F32)[None] * upper


def solution(mesh):
    in_specs = (
        P(None, "stream", "cy", "cz"),
        P(None, "stream", "cy", "cz"),
        P(None, "stream", "cy", "cz"),
        P(None, None, "stream", "cy", "cz"),
        P(),
        P("stream", "cy", "cz"),
        P("stream", "cy", "cz", None, None),
        P("stream", "cy", "cz", None),
        P("stream", "cy", "cz", None),
        P("stream", "cy", "cz", None, None),
        P("stream", "cy", "cz", None, None),
    )
    out_specs = P(None, "stream", "cy", "cz")
    return jax.shard_map(
        on_device, mesh=mesh, in_specs=in_specs, out_specs=out_specs, check_vma=False
    )
```

```python
import jax
import jax.numpy as jnp
from jax import lax
from jax.experimental import pallas as pl
from jax.experimental.pallas import tpu as pltpu
from jax.sharding import PartitionSpec as P

RELAX = 0.8
LANES = 128
F32 = jnp.float32
BF16 = jnp.bfloat16
VMEM = pl.BlockSpec(memory_space=pltpu.VMEM)
SMEM = pl.BlockSpec(memory_space=pltpu.SMEM)
BYTES = 24 << 20


def ring(x, axis, steps):
    count = lax.axis_size(axis)
    return lax.ppermute(x, axis, [(i, (i + steps) % count) for i in range(count)])


def call(kernel, outs, args, specs, name):
    return pl.pallas_call(
        kernel,
        out_shape=outs,
        in_specs=specs,
        out_specs=jax.tree.map(lambda _: VMEM, outs),
        name=name,
        compiler_params=pltpu.CompilerParams(vmem_limit_bytes=BYTES),
    )(*args)


def lane_pick(rows, lane):
    return jnp.take_along_axis(rows, lane, axis=1, mode="promise_in_bounds")


def donor_kernel(
    idx_hbm, count_hbm, state_hbm, out_ref, idx_ref, count_ref, state_ref, tab_ref, sems
):
    moves = [
        pltpu.make_async_copy(src, dst, sems.at[n])
        for n, (src, dst) in enumerate(
            ((count_hbm, count_ref), (state_hbm, state_ref), (idx_hbm, idx_ref))
        )
    ]
    for move in moves:
        move.start()
    for move in moves:
        move.wait()
    lanes = lax.broadcasted_iota(jnp.int32, (8, LANES), 1)
    subs = lax.broadcasted_iota(jnp.int32, (8, LANES), 0)
    lane_ids = lax.broadcasted_iota(jnp.int32, (LANES, 256), 0)
    slots = lax.broadcasted_iota(jnp.int32, (1, 256), 1)
    tab_ref[...] = jnp.zeros_like(tab_ref)
    for v in range(5):
        tab_ref[pl.ds(v, 32, stride=8), :] = state_ref[v * 32 : v * 32 + 32, :]
    whole = tab_ref[...]
    hi = whole.astype(BF16)
    tab = jnp.concatenate([hi, (whole - hi.astype(F32)).astype(BF16)], axis=1)
    for g in range(4):
        count = jnp.zeros((8, LANES), jnp.int32)
        for q in range(8):
            count = jnp.where(subs == q, count_ref[0, g * 8 + q], count)
        for h in range(2):
            idx = idx_ref[g * 8 : g * 8 + 8, h * LANES : (h + 1) * LANES]
            lane = idx & (LANES - 1)
            row = idx >> 7
            acc = [jnp.zeros((8, LANES), F32) for _ in range(5)]
            for r in range(32):
                hit = row == r
                for v in range(5):
                    line = state_ref[v * 32 + r : v * 32 + r + 1, :]
                    line = jnp.broadcast_to(line, (8, LANES))
                    acc[v] = jnp.where(hit, lane_pick(line, lane), acc[v])
            live = lanes + h * LANES < count
            for v in range(5):
                at = pl.ds(g * 80 + v * 2 + h, 8, stride=10)
                out_ref[at, :] = jnp.where(live, acc[v], 0.0)
        for d in range(32 + g * 8, 40 + g * 8):
            idx = idx_ref[d : d + 1, :]
            onehot = (lane_ids == (idx & (LANES - 1))).astype(BF16)
            onehot = jnp.concatenate([onehot, onehot], axis=0)
            p = jnp.dot(tab, onehot, preferred_element_type=F32)
            row = jnp.where(slots < count_ref[0, d], idx >> 7, -1)
            row = jnp.broadcast_to(row, (8, 256))
            acc = jnp.zeros((8, 256), F32)
            for r in range(32):
                acc = jnp.where(row == r, p[r * 8 : r * 8 + 8], acc)
            for h in range(2):
                at = pl.ds(d * 10 + h, 5, stride=2)
                out_ref[at, :] = acc[0:5, h * LANES : (h + 1) * LANES]


def coef(ref, d, i, j):
    return ref[25 * d + 5 * i + j : 25 * d + 5 * i + j + 1, :]


def stage_kernel(*refs):
    for src, dst in zip(refs[:4], refs[5:9]):
        dst[...] = src[...]
    couple_ref, coef_ref = refs[4], refs[9]
    for d in range(7):
        for i in range(5):
            for j in range(5):
                at = 25 * d + 5 * i + j
                coef_ref[at : at + 1, :] = jnp.full((1, LANES), couple_ref[d, i, j], F32)


def ghost_kernel(
    rec_ref, src_ref, w_ref, cell_ref, state_ref, f_ref, y_ref, z_ref
):
    his, los = [], []
    for v in range(5):
        t = jnp.concatenate(
            [rec_ref[pl.ds(v * 2 + h, 64, stride=10), :] for h in range(2)], axis=1
        )
        hi = t.astype(BF16)
        his.append(hi)
        los.append((t - hi.astype(F32)).astype(BF16))
    tab = jnp.concatenate(his + los, axis=0)
    width = 256
    lane_ids = lax.broadcasted_iota(jnp.int32, (256, width), 0)
    row_ids = lax.broadcasted_iota(jnp.int32, (64, width), 0)
    parts = [[] for _ in range(5)]
    tiles = [slice(t * LANES, (t + 1) * LANES) for t in (6, 7)]
    lane = [src_ref[:, t] & (LANES - 1) for t in tiles]
    line = [src_ref[:, t] >> 7 for t in tiles]
    found = [[jnp.zeros((8, LANES), F32) for _ in tiles] for _ in range(5)]
    for step in range(24):
        j, k = step // 8, step % 8
        if k == 0:
            acc = [jnp.zeros((8, width), F32) for _ in range(5)]
        at = slice(j * width, (j + 1) * width)
        entry = src_ref[k : k + 1, at]
        weight = w_ref[k : k + 1, at]
        onehot = (lane_ids == (entry & 255)).astype(BF16)
        p = jnp.dot(tab, onehot, preferred_element_type=F32)
        m = jnp.where(row_ids == (entry >> 8), weight, 0.0)
        for v in range(5):
            q = (p[64 * v : 64 * v + 64] + p[320 + 64 * v : 384 + 64 * v]) * m
            acc[v] = acc[v] + jnp.sum(q.reshape(8, 8, width), axis=0)
        for r in range(128 * step // 24, 128 * (step + 1) // 24):
            hit = [n == r for n in line]
            for v in range(5):
                at = (r // 2) * 10 + v * 2 + r % 2
                values = jnp.broadcast_to(rec_ref[at : at + 1, :], (8, LANES))
                for t in range(2):
                    found[v][t] = jnp.where(hit[t], lane_pick(values, lane[t]), found[v][t])
        if k == 7:
            for v in range(5):
                parts[v].append(jnp.sum(acc[v], axis=0, keepdims=True))
    for v in range(5):
        for t in range(2):
            weighted = found[v][t] * w_ref[:, tiles[t]]
            parts[v].append(jnp.sum(weighted, axis=0, keepdims=True))
    values = [jnp.concatenate(p, axis=1) for p in parts]

    cell = cell_ref[...]
    in_row = lax.broadcasted_iota(jnp.int32, (32, 1024), 0) == (cell >> 7)
    in_lane = lax.broadcasted_iota(jnp.int32, (LANES, 1024), 0) == (cell & (LANES - 1))
    pieces = [[], [], []]
    for v in range(5):
        x = jnp.where(in_row, values[v], 0.0)
        hi = x.astype(BF16)
        rest = x - hi.astype(F32)
        mid = rest.astype(BF16)
        pieces[0].append(hi)
        pieces[1].append(mid)
        pieces[2].append((rest - mid.astype(F32)).astype(BF16))
    left = jnp.concatenate([in_row.astype(BF16)] + pieces[0] + pieces[1] + pieces[2], axis=0)
    placed = lax.dot_general(
        left, in_lane.astype(BF16), (((1,), (1,)), ((), ())), preferred_element_type=F32
    )
    covered = placed[0:32] > 0.5
    diag = lax.broadcasted_iota(jnp.int32, (16, LANES), 0) == lax.broadcasted_iota(
        jnp.int32, (16, LANES), 1
    )
    for v in range(5):
        hi, mid, lo = (placed[32 * (1 + v + 5 * p) : 32 * (2 + v + 5 * p)] for p in range(3))
        old = state_ref[32 * v : 32 * v + 32, :]
        new = jnp.where(covered, hi + (mid + lo), old)
        f_ref[32 * v : 32 * v + 32, :] = new
        for x in range(2):
            plane = new[16 * x : 16 * x + 16]
            row = 2 * v + x
            y_ref[0, row : row + 1, :] = plane[0:1]
            y_ref[1, row : row + 1, :] = plane[15:16]
            for side, col in ((0, 0), (1, LANES - 1)):
                face = jnp.where(diag, plane[:, col : col + 1], 0.0)
                z_ref[side, row : row + 1, :] = jnp.sum(face, axis=0, keepdims=True)


def interior_kernel(f_ref, source_ref, scale_ref, couple_ref, out_ref):
    shape = (16, LANES)
    subs = lax.broadcasted_iota(jnp.int32, shape, 0)
    lanes = lax.broadcasted_iota(jnp.int32, shape, 1)
    for x in range(2):
        near = [[] for _ in range(6)]
        for v in range(5):
            mid = f_ref[32 * v + 16 * x : 32 * v + 16 * x + 16, :]
            near[0].append(mid)
            near[1].append(f_ref[32 * v + 16 * (1 - x) : 32 * v + 16 * (1 - x) + 16, :])
            near[2].append(jnp.where(subs == 0, 0.0, pltpu.roll(mid, 1, 0)))
            near[3].append(jnp.where(subs == 15, 0.0, pltpu.roll(mid, 15, 0)))
            near[4].append(jnp.where(lanes == 0, 0.0, pltpu.roll(mid, 1, 1)))
            near[5].append(jnp.where(lanes == LANES - 1, 0.0, pltpu.roll(mid, LANES - 1, 1)))
        for i in range(5):
            image = scale_ref[i, x] * near[0][i]
            for n, d in enumerate((0, 2 - x, 3, 4, 5, 6)):
                for j in range(5):
                    image = image + coef(couple_ref, d, i, j) * near[n][j]
            out_ref[x, i] = source_ref[i, x] - image


def residual_kernel(
    part_ref, f_ref, ym_ref, yp_ref, zm_ref, zp_ref, fluid_ref, couple_ref, same_ref, other_ref
):
    s, a, b = (lax.axis_index(n) for n in ("stream", "cy", "cz"))
    na, nb = (lax.axis_size(n) for n in ("cy", "cz"))
    half = lax.rem(s, 2)
    subs = lax.broadcasted_iota(jnp.int32, (8, LANES), 0)
    lanes = lax.broadcasted_iota(jnp.int32, (8, LANES), 1)

    def applied(d, ref, inside):
        rows = [jnp.where(inside, ref[2 * j : 2 * j + 2, :], 0.0) for j in range(5)]
        out = []
        for i in range(5):
            c = coef(couple_ref, d, i, 0) * rows[0]
            for j in range(1, 5):
                c = c + coef(couple_ref, d, i, j) * rows[j]
            out.append(c)
        return out

    ym, yp = applied(3, ym_ref, a > 0), applied(4, yp_ref, a < na - 1)
    zm, zp = applied(5, zm_ref, b > 0), applied(6, zp_ref, b < nb - 1)
    for x in range(2):
        for i in range(5):
            tiles, filled = [], []
            for t in range(2):
                r = part_ref[x, i, 8 * t : 8 * t + 8, :]
                edge = (ym if t == 0 else yp)[i][x : x + 1]
                r = r - jnp.where(subs == 7 * t, edge, 0.0)
                left, right = (
                    lane_pick(jnp.broadcast_to(z[i][x : x + 1], (8, LANES)), subs + 8 * t)
                    for z in (zm, zp)
                )
                r = r - jnp.where(lanes == 0, left, jnp.where(lanes == LANES - 1, right, 0.0))
                tiles.append(fluid_ref[x, 8 * t : 8 * t + 8, :].astype(F32) * r)
                at = 32 * i + 16 * x + 8 * t
                filled.append(f_ref[at : at + 8, :])
            for k, (first, second) in ((x, tiles), (2 + x, filled)):
                same_ref[k, i] = jnp.where(half == 0, first, second)
                other_ref[k, i] = jnp.where(half == 0, second, first)


def sweep_kernel(
    res_ref, prev_ref, next_ref, far_ref, inv_ref, couple_ref, mine_ref, theirs_ref, low_ref
):
    s = lax.axis_index("stream")
    pair = s + 1 - 2 * lax.rem(s, 2)
    count = 4
    zero = jnp.zeros((8, LANES), F32)
    offset = [lax.rem(q - s + count, count) for q in range(count)]

    def block(q, k):
        o = offset[q]
        return [
            jnp.where(
                o == 0,
                res_ref[k, i],
                jnp.where(
                    o == 1, next_ref[k, i], jnp.where(o == 2, far_ref[k, i], prev_ref[k, i])
                ),
            )
            for i in range(5)
        ]

    prev = [zero] * 5
    for q in range(count):
        o = offset[q]
        for x in range(2):
            t = block(q, x)
            wet = inv_ref[o, 25, x]
            if x == 0 and q > 0:
                prev = [p + wet * f for p, f in zip(prev, block(q - 1, 3))]
            if x == 1 and q < count - 1:
                ahead = block(q + 1, 2)
                for i in range(5):
                    c = coef(couple_ref, 2, i, 0) * ahead[0]
                    for j in range(1, 5):
                        c = c + coef(couple_ref, 2, i, j) * ahead[j]
                    t[i] = t[i] - wet * c
            for i in range(5):
                for j in range(5):
                    t[i] = t[i] - coef(couple_ref, 1, i, j) * prev[j]
            cur = []
            for i in range(5):
                c = inv_ref[o, 5 * i, x] * t[0]
                for j in range(1, 5):
                    c = c + inv_ref[o, 5 * i + j, x] * t[j]
                cur.append(c)
                low_ref[2 * q + x, i] = c
            prev = cur
    prev = [zero] * 5
    for q in reversed(range(count)):
        o = offset[q]
        for x in (1, 0):
            t = []
            for i in range(5):
                r = coef(couple_ref, 2, i, 0) * prev[0]
                for j in range(1, 5):
                    r = r + coef(couple_ref, 2, i, j) * prev[j]
                t.append(r)
            cur = []
            for i in range(5):
                c = low_ref[2 * q + x, i]
                for j in range(5):
                    c = c - inv_ref[o, 5 * i + j, x] * t[j]
                cur.append(c)
            prev = cur
            for where, to_ref in ((s, mine_ref), (pair, theirs_ref)):

                @pl.when(where == q)
                def _():
                    for i in range(5):
                        to_ref[i, x] = cur[i]


def on_device(
    state,
    source,
    diag_scale,
    diag_inverse,
    couple,
    fluid,
    donor_index,
    donor_count,
    ghost_cell,
    ghost_source,
    ghost_weight,
):
    table = state.reshape(160, LANES)
    sent = pl.pallas_call(
        donor_kernel,
        out_shape=jax.ShapeDtypeStruct((640, LANES), F32),
        in_specs=[pl.BlockSpec(memory_space=pl.ANY)] * 3,
        out_specs=VMEM,
        scratch_shapes=[
            pltpu.VMEM((64, 256), jnp.int32),
            pltpu.SMEM((1, 64), jnp.int32),
            pltpu.VMEM((160, LANES), F32),
            pltpu.VMEM((256, LANES), F32),
            pltpu.SemaphoreType.DMA((3,)),
        ],
        name="donor_pick",
        compiler_params=pltpu.CompilerParams(vmem_limit_bytes=60 << 20),
    )(donor_index.reshape(64, 256), donor_count.reshape(1, 64), table)
    lists = (
        ghost_source.reshape(1024, 8).T,
        ghost_weight.reshape(1024, 8).T,
        ghost_cell.reshape(1, 1024),
        table,
    )
    entries, weights, cells, table, coefs = call(
        stage_kernel,
        tuple(jax.ShapeDtypeStruct(x.shape, x.dtype) for x in lists)
        + (jax.ShapeDtypeStruct((175, LANES), F32),),
        lists + (couple,),
        [VMEM] * 4 + [SMEM],
        "stage_lists",
    )
    sent = sent.reshape(64, 1, 1280)
    received = lax.all_to_all(sent, ("cy", "cz"), split_axis=0, concat_axis=0, tiled=True)
    half = lax.rem(lax.axis_index("stream"), 2)
    frozen = jnp.concatenate([diag_inverse.reshape(25, 2, 16, LANES), fluid.astype(F32)[None]])
    inv_same, inv_other = (
        lax.dynamic_slice_in_dim(frozen, 8 * h, 8, 2) for h in (half, 1 - half)
    )
    inv_prev, inv_next = ring(inv_other, "stream", 1), ring(inv_other, "stream", -1)
    inv_far = ring(inv_same, "stream", 2)
    faces = jax.ShapeDtypeStruct((2, 10, LANES), F32)
    filled, yface, zface = call(
        ghost_kernel,
        (jax.ShapeDtypeStruct((160, LANES), F32), faces, faces),
        (
            received.reshape(640, LANES),
            entries,
            weights,
            cells,
            table,
        ),
        [VMEM] * 5,
        "ghost_fill",
    )
    filled, yface, zface, inv_prev, inv_next, inv_far = lax.optimization_barrier(
        (filled, yface, zface, inv_prev, inv_next, inv_far)
    )
    inv = jnp.stack([inv_same, inv_next, inv_far, inv_prev])
    ym, yp = ring(yface[1], "cy", 1), ring(yface[0], "cy", -1)
    zm, zp = ring(zface[1], "cz", 1), ring(zface[0], "cz", -1)
    part = jax.ShapeDtypeStruct((4, 5, 8, LANES), F32)
    inside = call(
        interior_kernel,
        jax.ShapeDtypeStruct((2, 5, 16, LANES), F32),
        (filled, source, diag_scale, coefs),
        [VMEM] * 4,
        "interior",
    )
    same, other = call(
        residual_kernel,
        (part, part),
        (inside, filled, ym, yp, zm, zp, fluid, coefs),
        [VMEM] * 7 + [VMEM],
        "residual",
    )
    before, after = ring(other, "stream", 1), ring(other, "stream", -1)
    far = ring(same, "stream", 2)
    part = jax.ShapeDtypeStruct((5, 2, 8, LANES), F32)
    mine, theirs = pl.pallas_call(
        sweep_kernel,
        out_shape=(part, part),
        in_specs=[VMEM] * 6,
        out_specs=(VMEM, VMEM),
        scratch_shapes=[pltpu.VMEM((8, 5, 8, LANES), F32)],
        name="sweeps",
        compiler_params=pltpu.CompilerParams(vmem_limit_bytes=BYTES),
    )(same, before, after, far, inv, coefs)
    swapped = lax.ppermute(
        theirs, "stream", [(i, i ^ 1) for i in range(lax.axis_size("stream"))]
    )
    first_half = jnp.where(half == 0, mine, swapped)
    second_half = jnp.where(half == 0, swapped, mine)
    upper = jnp.concatenate([first_half, second_half], axis=2)
    return filled.reshape(5, 2, 16, LANES) + RELAX * fluid.astype(F32)[None] * upper


def solution(mesh):
    in_specs = (
        P(None, "stream", "cy", "cz"),
        P(None, "stream", "cy", "cz"),
        P(None, "stream", "cy", "cz"),
        P(None, None, "stream", "cy", "cz"),
        P(),
        P("stream", "cy", "cz"),
        P("stream", "cy", "cz", None, None),
        P("stream", "cy", "cz", None),
        P("stream", "cy", "cz", None),
        P("stream", "cy", "cz", None, None),
        P("stream", "cy", "cz", None, None),
    )
    out_specs = P(None, "stream", "cy", "cz")
    return jax.shard_map(
        on_device, mesh=mesh, in_specs=in_specs, out_specs=out_specs, check_vma=False
    )
```

```python
import jax
import jax.numpy as jnp
from jax import lax
from jax.experimental import pallas as pl
from jax.experimental.pallas import tpu as pltpu
from jax.sharding import PartitionSpec as P

RELAX = 0.8
LANES = 128
F32 = jnp.float32
BF16 = jnp.bfloat16
VMEM = pl.BlockSpec(memory_space=pltpu.VMEM)
SMEM = pl.BlockSpec(memory_space=pltpu.SMEM)
BYTES = 24 << 20


def ring(x, axis, steps):
    count = lax.axis_size(axis)
    return lax.ppermute(x, axis, [(i, (i + steps) % count) for i in range(count)])


def call(kernel, outs, args, specs, name):
    return pl.pallas_call(
        kernel,
        out_shape=outs,
        in_specs=specs,
        out_specs=jax.tree.map(lambda _: VMEM, outs),
        name=name,
        compiler_params=pltpu.CompilerParams(vmem_limit_bytes=BYTES),
    )(*args)


def lane_pick(rows, lane):
    return jnp.take_along_axis(rows, lane, axis=1, mode="promise_in_bounds")


def donor_kernel(
    idx_hbm, count_hbm, state_hbm, out_ref, idx_ref, count_ref, state_ref, tab_ref, sems
):
    moves = [
        pltpu.make_async_copy(src, dst, sems.at[n])
        for n, (src, dst) in enumerate(
            ((count_hbm, count_ref), (state_hbm, state_ref), (idx_hbm, idx_ref))
        )
    ]
    for move in moves:
        move.start()
    for move in moves:
        move.wait()
    lanes = lax.broadcasted_iota(jnp.int32, (8, LANES), 1)
    subs = lax.broadcasted_iota(jnp.int32, (8, LANES), 0)
    lane_ids = lax.broadcasted_iota(jnp.int32, (LANES, 256), 0)
    slots = lax.broadcasted_iota(jnp.int32, (1, 256), 1)
    tab_ref[...] = jnp.zeros_like(tab_ref)
    for v in range(5):
        tab_ref[pl.ds(v, 32, stride=8), :] = state_ref[v * 32 : v * 32 + 32, :]
    whole = tab_ref[...]
    hi = whole.astype(BF16)
    tab = jnp.concatenate([hi, (whole - hi.astype(F32)).astype(BF16)], axis=1)
    for g in range(4):
        count = jnp.zeros((8, LANES), jnp.int32)
        for q in range(8):
            count = jnp.where(subs == q, count_ref[0, g * 8 + q], count)
        for h in range(2):
            idx = idx_ref[g * 8 : g * 8 + 8, h * LANES : (h + 1) * LANES]
            lane = idx & (LANES - 1)
            row = idx >> 7
            acc = [jnp.zeros((8, LANES), F32) for _ in range(5)]
            for r in range(32):
                hit = row == r
                for v in range(5):
                    line = state_ref[v * 32 + r : v * 32 + r + 1, :]
                    line = jnp.broadcast_to(line, (8, LANES))
                    acc[v] = jnp.where(hit, lane_pick(line, lane), acc[v])
            live = lanes + h * LANES < count
            for v in range(5):
                at = pl.ds(g * 80 + v * 2 + h, 8, stride=10)
                out_ref[at, :] = jnp.where(live, acc[v], 0.0)
        for d in range(32 + g * 8, 40 + g * 8):
            idx = idx_ref[d : d + 1, :]
            onehot = (lane_ids == (idx & (LANES - 1))).astype(BF16)
            onehot = jnp.concatenate([onehot, onehot], axis=0)
            p = jnp.dot(tab, onehot, preferred_element_type=F32)
            row = jnp.where(slots < count_ref[0, d], idx >> 7, -1)
            row = jnp.broadcast_to(row, (8, 256))
            acc = jnp.zeros((8, 256), F32)
            for r in range(32):
                acc = jnp.where(row == r, p[r * 8 : r * 8 + 8], acc)
            for h in range(2):
                at = pl.ds(d * 10 + h, 5, stride=2)
                out_ref[at, :] = acc[0:5, h * LANES : (h + 1) * LANES]


def coef(ref, d, i, j):
    return ref[25 * d + 5 * i + j : 25 * d + 5 * i + j + 1, :]


def stage_kernel(*refs):
    for src, dst in zip(refs[:4], refs[5:9]):
        dst[...] = src[...]
    couple_ref, coef_ref = refs[4], refs[9]
    for d in range(7):
        for i in range(5):
            for j in range(5):
                at = 25 * d + 5 * i + j
                coef_ref[at : at + 1, :] = jnp.full((1, LANES), couple_ref[d, i, j], F32)


def ghost_kernel(
    rec_ref, src_ref, w_ref, cell_ref, state_ref, f_ref, y_ref, z_ref
):
    his, los = [], []
    for v in range(5):
        t = jnp.concatenate(
            [rec_ref[pl.ds(v * 2 + h, 64, stride=10), :] for h in range(2)], axis=1
        )
        hi = t.astype(BF16)
        his.append(hi)
        los.append((t - hi.astype(F32)).astype(BF16))
    tab = jnp.concatenate(his + los, axis=0)
    width = 256
    lane_ids = lax.broadcasted_iota(jnp.int32, (256, width), 0)
    row_ids = lax.broadcasted_iota(jnp.int32, (64, width), 0)
    parts = [[] for _ in range(5)]
    tiles = [slice(t * LANES, (t + 1) * LANES) for t in (6, 7)]
    lane = [src_ref[:, t] & (LANES - 1) for t in tiles]
    line = [src_ref[:, t] >> 7 for t in tiles]
    found = [[jnp.zeros((8, LANES), F32) for _ in tiles] for _ in range(5)]
    for step in range(24):
        j, k = step // 8, step % 8
        if k == 0:
            acc = [jnp.zeros((8, width), F32) for _ in range(5)]
        at = slice(j * width, (j + 1) * width)
        entry = src_ref[k : k + 1, at]
        weight = w_ref[k : k + 1, at]
        onehot = (lane_ids == (entry & 255)).astype(BF16)
        p = jnp.dot(tab, onehot, preferred_element_type=F32)
        m = jnp.where(row_ids == (entry >> 8), weight, 0.0)
        for v in range(5):
            q = (p[64 * v : 64 * v + 64] + p[320 + 64 * v : 384 + 64 * v]) * m
            acc[v] = acc[v] + jnp.sum(q.reshape(8, 8, width), axis=0)
        for r in range(128 * step // 24, 128 * (step + 1) // 24):
            hit = [n == r for n in line]
            for v in range(5):
                at = (r // 2) * 10 + v * 2 + r % 2
                values = jnp.broadcast_to(rec_ref[at : at + 1, :], (8, LANES))
                for t in range(2):
                    found[v][t] = jnp.where(hit[t], lane_pick(values, lane[t]), found[v][t])
        if k == 7:
            for v in range(5):
                parts[v].append(jnp.sum(acc[v], axis=0, keepdims=True))
    for v in range(5):
        for t in range(2):
            weighted = found[v][t] * w_ref[:, tiles[t]]
            parts[v].append(jnp.sum(weighted, axis=0, keepdims=True))
    values = [jnp.concatenate(p, axis=1) for p in parts]

    cell = cell_ref[...]
    in_row = lax.broadcasted_iota(jnp.int32, (32, 1024), 0) == (cell >> 7)
    in_lane = lax.broadcasted_iota(jnp.int32, (LANES, 1024), 0) == (cell & (LANES - 1))
    pieces = [[], []]
    for v in range(5):
        x = jnp.where(in_row, values[v], 0.0)
        hi = x.astype(BF16)
        pieces[0].append(hi)
        pieces[1].append((x - hi.astype(F32)).astype(BF16))
    left = jnp.concatenate([in_row.astype(BF16)] + pieces[0] + pieces[1], axis=0)
    placed = lax.dot_general(
        left, in_lane.astype(BF16), (((1,), (1,)), ((), ())), preferred_element_type=F32
    )
    covered = placed[0:32] > 0.5
    diag = lax.broadcasted_iota(jnp.int32, (16, LANES), 0) == lax.broadcasted_iota(
        jnp.int32, (16, LANES), 1
    )
    for v in range(5):
        hi, lo = (placed[32 * (1 + v + 5 * p) : 32 * (2 + v + 5 * p)] for p in range(2))
        old = state_ref[32 * v : 32 * v + 32, :]
        new = jnp.where(covered, hi + lo, old)
        f_ref[32 * v : 32 * v + 32, :] = new
        for x in range(2):
            plane = new[16 * x : 16 * x + 16]
            row = 2 * v + x
            y_ref[0, row : row + 1, :] = plane[0:1]
            y_ref[1, row : row + 1, :] = plane[15:16]
            for side, col in ((0, 0), (1, LANES - 1)):
                face = jnp.where(diag, plane[:, col : col + 1], 0.0)
                z_ref[side, row : row + 1, :] = jnp.sum(face, axis=0, keepdims=True)


def interior_kernel(f_ref, source_ref, scale_ref, couple_ref, out_ref):
    shape = (16, LANES)
    subs = lax.broadcasted_iota(jnp.int32, shape, 0)
    lanes = lax.broadcasted_iota(jnp.int32, shape, 1)
    for x in range(2):
        near = [[] for _ in range(6)]
        for v in range(5):
            mid = f_ref[32 * v + 16 * x : 32 * v + 16 * x + 16, :]
            near[0].append(mid)
            near[1].append(f_ref[32 * v + 16 * (1 - x) : 32 * v + 16 * (1 - x) + 16, :])
            near[2].append(jnp.where(subs == 0, 0.0, pltpu.roll(mid, 1, 0)))
            near[3].append(jnp.where(subs == 15, 0.0, pltpu.roll(mid, 15, 0)))
            near[4].append(jnp.where(lanes == 0, 0.0, pltpu.roll(mid, 1, 1)))
            near[5].append(jnp.where(lanes == LANES - 1, 0.0, pltpu.roll(mid, LANES - 1, 1)))
        for i in range(5):
            image = scale_ref[i, x] * near[0][i]
            for n, d in enumerate((0, 2 - x, 3, 4, 5, 6)):
                for j in range(5):
                    image = image + coef(couple_ref, d, i, j) * near[n][j]
            out_ref[x, i] = source_ref[i, x] - image


def residual_kernel(
    part_ref, f_ref, ym_ref, yp_ref, zm_ref, zp_ref, fluid_ref, couple_ref, same_ref, other_ref
):
    s, a, b = (lax.axis_index(n) for n in ("stream", "cy", "cz"))
    na, nb = (lax.axis_size(n) for n in ("cy", "cz"))
    half = lax.rem(s, 2)
    subs = lax.broadcasted_iota(jnp.int32, (8, LANES), 0)
    lanes = lax.broadcasted_iota(jnp.int32, (8, LANES), 1)

    def applied(d, ref, inside):
        rows = [jnp.where(inside, ref[2 * j : 2 * j + 2, :], 0.0) for j in range(5)]
        out = []
        for i in range(5):
            c = coef(couple_ref, d, i, 0) * rows[0]
            for j in range(1, 5):
                c = c + coef(couple_ref, d, i, j) * rows[j]
            out.append(c)
        return out

    ym, yp = applied(3, ym_ref, a > 0), applied(4, yp_ref, a < na - 1)
    zm, zp = applied(5, zm_ref, b > 0), applied(6, zp_ref, b < nb - 1)
    for x in range(2):
        for i in range(5):
            tiles, filled = [], []
            for t in range(2):
                r = part_ref[x, i, 8 * t : 8 * t + 8, :]
                edge = (ym if t == 0 else yp)[i][x : x + 1]
                r = r - jnp.where(subs == 7 * t, edge, 0.0)
                left, right = (
                    lane_pick(jnp.broadcast_to(z[i][x : x + 1], (8, LANES)), subs + 8 * t)
                    for z in (zm, zp)
                )
                r = r - jnp.where(lanes == 0, left, jnp.where(lanes == LANES - 1, right, 0.0))
                tiles.append(fluid_ref[x, 8 * t : 8 * t + 8, :].astype(F32) * r)
                at = 32 * i + 16 * x + 8 * t
                filled.append(f_ref[at : at + 8, :])
            for k, (first, second) in ((x, tiles), (2 + x, filled)):
                same_ref[k, i] = jnp.where(half == 0, first, second)
                other_ref[k, i] = jnp.where(half == 0, second, first)


def sweep_kernel(
    res_ref, prev_ref, next_ref, far_ref, inv_ref, couple_ref, mine_ref, theirs_ref, low_ref
):
    s = lax.axis_index("stream")
    pair = s + 1 - 2 * lax.rem(s, 2)
    count = 4
    zero = jnp.zeros((8, LANES), F32)
    offset = [lax.rem(q - s + count, count) for q in range(count)]

    def block(q, k):
        o = offset[q]
        return [
            jnp.where(
                o == 0,
                res_ref[k, i],
                jnp.where(
                    o == 1, next_ref[k, i], jnp.where(o == 2, far_ref[k, i], prev_ref[k, i])
                ),
            )
            for i in range(5)
        ]

    prev = [zero] * 5
    for q in range(count):
        o = offset[q]
        for x in range(2):
            t = block(q, x)
            wet = inv_ref[o, 25, x]
            if x == 0 and q > 0:
                prev = [p + wet * f for p, f in zip(prev, block(q - 1, 3))]
            if x == 1 and q < count - 1:
                ahead = block(q + 1, 2)
                for i in range(5):
                    c = coef(couple_ref, 2, i, 0) * ahead[0]
                    for j in range(1, 5):
                        c = c + coef(couple_ref, 2, i, j) * ahead[j]
                    t[i] = t[i] - wet * c
            for i in range(5):
                for j in range(5):
                    t[i] = t[i] - coef(couple_ref, 1, i, j) * prev[j]
            cur = []
            for i in range(5):
                c = inv_ref[o, 5 * i, x] * t[0]
                for j in range(1, 5):
                    c = c + inv_ref[o, 5 * i + j, x] * t[j]
                cur.append(c)
                low_ref[2 * q + x, i] = c
            prev = cur
    prev = [zero] * 5
    for q in reversed(range(count)):
        o = offset[q]
        for x in (1, 0):
            t = []
            for i in range(5):
                r = coef(couple_ref, 2, i, 0) * prev[0]
                for j in range(1, 5):
                    r = r + coef(couple_ref, 2, i, j) * prev[j]
                t.append(r)
            cur = []
            for i in range(5):
                c = low_ref[2 * q + x, i]
                for j in range(5):
                    c = c - inv_ref[o, 5 * i + j, x] * t[j]
                cur.append(c)
            prev = cur
            for where, to_ref in ((s, mine_ref), (pair, theirs_ref)):

                @pl.when(where == q)
                def _():
                    for i in range(5):
                        to_ref[i, x] = cur[i]


def on_device(
    state,
    source,
    diag_scale,
    diag_inverse,
    couple,
    fluid,
    donor_index,
    donor_count,
    ghost_cell,
    ghost_source,
    ghost_weight,
):
    table = state.reshape(160, LANES)
    sent = pl.pallas_call(
        donor_kernel,
        out_shape=jax.ShapeDtypeStruct((640, LANES), F32),
        in_specs=[pl.BlockSpec(memory_space=pl.ANY)] * 3,
        out_specs=VMEM,
        scratch_shapes=[
            pltpu.VMEM((64, 256), jnp.int32),
            pltpu.SMEM((1, 64), jnp.int32),
            pltpu.VMEM((160, LANES), F32),
            pltpu.VMEM((256, LANES), F32),
            pltpu.SemaphoreType.DMA((3,)),
        ],
        name="donor_pick",
        compiler_params=pltpu.CompilerParams(vmem_limit_bytes=60 << 20),
    )(donor_index.reshape(64, 256), donor_count.reshape(1, 64), table)
    lists = (
        ghost_source.reshape(1024, 8).T,
        ghost_weight.reshape(1024, 8).T,
        ghost_cell.reshape(1, 1024),
        table,
    )
    entries, weights, cells, table, coefs = call(
        stage_kernel,
        tuple(jax.ShapeDtypeStruct(x.shape, x.dtype) for x in lists)
        + (jax.ShapeDtypeStruct((175, LANES), F32),),
        lists + (couple,),
        [VMEM] * 4 + [SMEM],
        "stage_lists",
    )
    sent = sent.reshape(64, 1, 1280)
    received = lax.all_to_all(sent, ("cy", "cz"), split_axis=0, concat_axis=0, tiled=True)
    half = lax.rem(lax.axis_index("stream"), 2)
    frozen = jnp.concatenate([diag_inverse.reshape(25, 2, 16, LANES), fluid.astype(F32)[None]])
    inv_same, inv_other = (
        lax.dynamic_slice_in_dim(frozen, 8 * h, 8, 2) for h in (half, 1 - half)
    )
    inv_prev, inv_next = ring(inv_other, "stream", 1), ring(inv_other, "stream", -1)
    inv_far = ring(inv_same, "stream", 2)
    faces = jax.ShapeDtypeStruct((2, 10, LANES), F32)
    filled, yface, zface = call(
        ghost_kernel,
        (jax.ShapeDtypeStruct((160, LANES), F32), faces, faces),
        (
            received.reshape(640, LANES),
            entries,
            weights,
            cells,
            table,
        ),
        [VMEM] * 5,
        "ghost_fill",
    )
    filled, yface, zface, inv_prev, inv_next, inv_far = lax.optimization_barrier(
        (filled, yface, zface, inv_prev, inv_next, inv_far)
    )
    inv = jnp.stack([inv_same, inv_next, inv_far, inv_prev])
    ym, yp = ring(yface[1], "cy", 1), ring(yface[0], "cy", -1)
    zm, zp = ring(zface[1], "cz", 1), ring(zface[0], "cz", -1)
    part = jax.ShapeDtypeStruct((4, 5, 8, LANES), F32)
    inside = call(
        interior_kernel,
        jax.ShapeDtypeStruct((2, 5, 16, LANES), F32),
        (filled, source, diag_scale, coefs),
        [VMEM] * 4,
        "interior",
    )
    same, other = call(
        residual_kernel,
        (part, part),
        (inside, filled, ym, yp, zm, zp, fluid, coefs),
        [VMEM] * 7 + [VMEM],
        "residual",
    )
    before, after = ring(other, "stream", 1), ring(other, "stream", -1)
    far = ring(same, "stream", 2)
    part = jax.ShapeDtypeStruct((5, 2, 8, LANES), F32)
    mine, theirs = pl.pallas_call(
        sweep_kernel,
        out_shape=(part, part),
        in_specs=[VMEM] * 6,
        out_specs=(VMEM, VMEM),
        scratch_shapes=[pltpu.VMEM((8, 5, 8, LANES), F32)],
        name="sweeps",
        compiler_params=pltpu.CompilerParams(vmem_limit_bytes=BYTES),
    )(same, before, after, far, inv, coefs)
    swapped = lax.ppermute(
        theirs, "stream", [(i, i ^ 1) for i in range(lax.axis_size("stream"))]
    )
    first_half = jnp.where(half == 0, mine, swapped)
    second_half = jnp.where(half == 0, swapped, mine)
    upper = jnp.concatenate([first_half, second_half], axis=2)
    return filled.reshape(5, 2, 16, LANES) + RELAX * fluid.astype(F32)[None] * upper


def solution(mesh):
    in_specs = (
        P(None, "stream", "cy", "cz"),
        P(None, "stream", "cy", "cz"),
        P(None, "stream", "cy", "cz"),
        P(None, None, "stream", "cy", "cz"),
        P(),
        P("stream", "cy", "cz"),
        P("stream", "cy", "cz", None, None),
        P("stream", "cy", "cz", None),
        P("stream", "cy", "cz", None),
        P("stream", "cy", "cz", None, None),
        P("stream", "cy", "cz", None, None),
    )
    out_specs = P(None, "stream", "cy", "cz")
    return jax.shard_map(
        on_device, mesh=mesh, in_specs=in_specs, out_specs=out_specs, check_vma=False
    )
```
